32 devices in a mesh: tok: 4 (over z), head: 8 (over y, x, core).
Axes of the slice: x: 2, y: 2, z: 4, core: 2. Of those that a mesh axis runs over, the one named last changes fastest.
Arguments:
- stream: bfloat16 [1024, 7168], P('tok'), may hold values from -400 to 400
- row_tree_nodes: int32 [1024], replicated, may hold values from 0 to 1023, as said below
- input_norm_gain: bfloat16 [7168], replicated, may hold values from 0.099609375 to 1.8984375
- query_key_value_weight: bfloat16 [7168, 3, 7168], P('head', None, 'tok'), may hold values from -0.141736677 to 0.141736677
- adapter_down_weight: bfloat16 [7168, 128], replicated, may hold values from -0.0625 to 0.0625
- adapter_up_weight: bfloat16 [128, 3, 7168], P('head', None, 'tok'), may hold values from -0.23925781 to 0.23925781
- key_value_cache: bfloat16 [2, 16, 2048, 7168], P(None, 'head', None, 'tok'), may hold values from -104 to 104
- cache_length: int32 [16], P('head'), may hold values from 256 to 2048, as said below
- parents: int32 [16, 64], P('head'), may hold values from 0 to 62, as said below
- accepted: int32 [16, 8], P('head'), may hold values from 0 to 63, as said below
- output_weight: bfloat16 [7168, 3584], P('tok', 'head'), may hold values from -0.375 to 0.375
Outputs:
- attended: bfloat16 [1024, 3584], P('tok', 'head')
- accepted_kv: bfloat16 [2, 16, 8, 7168], P(None, 'head', None, 'tok')
The draws below stay inside these ranges and needn't reach their ends.
Inputs may be any that keep to these rules, and one draw needn't show every extreme that they name: row_tree_nodes is a permutation of the 1024 node numbers; every aligned block of 128 rows holds exactly 8 nodes of every request. `cache_length`: at least one request's cache holds exactly 2048 positions. parents[r, 0] = 0 marks the root; parents[r, n] < n for n > 0. `accepted`: each row lists 8 nodes of its request's tree, each the parent of the next.
All inputs are finite; a program needn't handle non-finite values.
Results may differ from the reference program's by a relative error of at most 0.014.
Values may be sent and summed in bfloat16 or wider, within the bound.
No kernel may reach another device: no remote copies, remote signals or barrier semaphores. Data moves between devices by JAX's collectives and lax.ppermute only.
A program may use at most 192 MiB of HBM per device.

```python
import math
import jax
import jax.numpy as jnp
from jax import lax

D = 3584
HEAD_COUNT = 32
HEAD_SIZE = 224
ADAPTER_RANK = 128
NODES = 64
DEPTH = 8
REQ_DEV = 2
CACHE = 2048
INPUT_WIDTH = 7168
REQ = 16
TOKENS = 1024


def draw_stream(key, part):
    base_key, row_key, column_key = jax.random.split(key, 3)
    row_scale = jnp.exp(jax.random.uniform(row_key, (TOKENS, 1), jnp.float32, 0.0, math.log(10.0)))
    column_scale = jnp.exp(jax.random.uniform(column_key, (1, INPUT_WIDTH), jnp.float32, 0.0, math.log(10.0)))
    core = jnp.clip(jax.random.normal(base_key, (TOKENS, INPUT_WIDTH), jnp.float32), -4.0, 4.0)
    return (core * row_scale * column_scale).astype(jnp.bfloat16)


def draw_row_tree_nodes(key, part):
    owners = REQ // REQ_DEV
    share_count = NODES // owners
    order_key, shuffle_key = jax.random.split(key)
    orders = jax.vmap(lambda one_key: jax.random.permutation(one_key, NODES))(jax.random.split(order_key, REQ))
    node_ids = orders.astype(jnp.int32) + (jnp.arange(REQ, dtype=jnp.int32) * NODES)[:, None]
    grouped = node_ids.reshape(REQ, owners, share_count).transpose(1, 0, 2).reshape(owners, REQ * share_count)
    shuffles = jax.vmap(lambda one_key: jax.random.permutation(one_key, REQ * share_count))(jax.random.split(shuffle_key, owners))
    return jnp.take_along_axis(grouped, shuffles.astype(jnp.int32), axis=1).reshape(TOKENS).astype(jnp.int32)


def draw_query_key_value_weight(key, part):
    slot_scale = jnp.array([1.0, 3.0, 1.0], jnp.float32)[None, :, None] * INPUT_WIDTH ** (-0.5)
    base = jnp.clip(jax.random.normal(key, (INPUT_WIDTH, 3, HEAD_COUNT * HEAD_SIZE), jnp.float32), -4.0, 4.0)
    return (base * slot_scale).astype(jnp.bfloat16)


def draw_key_value_cache(key, part):
    key_key, value_key = jax.random.split(key, 2)
    target_shape = (REQ, CACHE, HEAD_COUNT * HEAD_SIZE)
    keys_part = jnp.clip(jax.random.normal(key_key, target_shape, jnp.float32), -4.0, 4.0)
    values_part = jnp.clip(jax.random.normal(value_key, target_shape, jnp.float32), -4.0, 4.0)
    return jnp.stack([keys_part, values_part]).astype(jnp.bfloat16)


def draw_cache_length(key, part):
    length_key, full_key = jax.random.split(key)
    lengths = jax.random.randint(length_key, (REQ,), CACHE // 8, CACHE + 1)
    full_slot = jax.random.randint(full_key, (), 0, REQ)
    return jnp.where(jnp.arange(REQ) == full_slot, CACHE, lengths).astype(jnp.int32)


def tree_walk(key):
    tree_key = jax.random.fold_in(key, 11)
    back_key, leaf_key = jax.random.split(tree_key)
    steps_back = jax.random.randint(back_key, (REQ, NODES), 0, 4)
    positions = jnp.arange(NODES, dtype=jnp.int32)[None, :]
    parent_table = jnp.maximum(positions - 1 - steps_back, 0).astype(jnp.int32)
    leaves = jax.random.randint(leaf_key, (REQ,), NODES - 4, NODES).astype(jnp.int32)
    path_nodes = [leaves]
    for depth_step in range(DEPTH - 1):
        path_nodes.append(jnp.take_along_axis(parent_table, path_nodes[-1][:, None], axis=1)[:, 0])
    accepted_path = jnp.stack(path_nodes[::-1], axis=1).astype(jnp.int32)
    return (parent_table, accepted_path)


def draw_parents(key, part):
    return tree_walk(key)[0]


def draw_accepted(key, part):
    return tree_walk(key)[1]


def block_scale(stream_key, shape, cuts, smallest, high):
    level = 1.0
    for axis_at, parts in cuts:
        steps = jax.random.uniform(jax.random.fold_in(jax.random.fold_in(stream_key, 6), axis_at), (parts,), jnp.float32, smallest / len(cuts), high / len(cuts))
        level = level * jnp.repeat(jnp.exp(steps), shape[axis_at] // parts).reshape((-1,) + (1,) * (len(shape) - 1 - axis_at))
    return level


def bell_draw(own_key, shape, width, most, cuts=(), kind=jnp.bfloat16):
    result = jax.random.normal(own_key, shape, jnp.float32) * width
    if len(cuts) > 0:
        result = block_scale(own_key, shape, cuts, -0.22, 0.18) * result
    return jnp.clip(result, min=-most, max=most).astype(kind)


def setup_inputs(seed: int = 0) -> dict:
    key_list = jax.random.split(jax.random.key(seed), 12)
    return {
        "stream": draw_stream(jax.random.fold_in(key_list[11], 71), 0),
        "row_tree_nodes": draw_row_tree_nodes(jax.random.fold_in(key_list[11], 71), 0),
        "input_norm_gain": jnp.clip(1.0 + 0.18 * jax.random.normal(key_list[2], (INPUT_WIDTH,), jnp.float32), 0.099609375, 1.8984375).astype(jnp.bfloat16),
        "query_key_value_weight": draw_query_key_value_weight(jax.random.fold_in(key_list[11], 71), 0),
        "adapter_down_weight": bell_draw(key_list[4], (INPUT_WIDTH, ADAPTER_RANK), INPUT_WIDTH ** -0.5, 0.0625),
        "adapter_up_weight": bell_draw(key_list[5], (ADAPTER_RANK, 3, HEAD_COUNT * HEAD_SIZE), 0.04, 0.23925781, ((0, 8), (2, 4))),
        "key_value_cache": draw_key_value_cache(jax.random.fold_in(key_list[11], 71), 0),
        "cache_length": draw_cache_length(jax.random.fold_in(key_list[11], 71), 0),
        "parents": draw_parents(jax.random.fold_in(key_list[11], 71), 0),
        "accepted": draw_accepted(jax.random.fold_in(key_list[11], 71), 0),
        "output_weight": bell_draw(key_list[10], (HEAD_COUNT * HEAD_SIZE, D), HEAD_SIZE ** -0.5, 0.375, ((0, 4), (1, 8))),
    }


def ancestors_of(parents):
    parent_links = jax.nn.one_hot(parents, NODES, dtype=jnp.float32)
    identity_matrix = jnp.eye(NODES, dtype=jnp.float32)
    ancestry = jnp.minimum(identity_matrix[None] + parent_links, 1.0)
    for squaring in range(NODES.bit_length()):
        ancestry = jnp.minimum(jnp.einsum('rnm,rmk->rnk', ancestry, ancestry, precision=lax.Precision.HIGHEST), 1.0)
    return ancestry

def attend_one(request_item):
    queries, tree_key_rows, tree_value_rows, keys_cache, values_cache, length, ancestry = request_item
    attention_score_scale = HEAD_SIZE ** (-0.5)
    query_full_rows = queries.astype(jnp.float32)
    cache_scores = jnp.einsum('nhd,chd->hnc', query_full_rows, keys_cache.astype(jnp.float32)) * attention_score_scale
    live_mask = jnp.arange(CACHE) < length
    cache_scores = jnp.where(live_mask[None, None, :], cache_scores, -jnp.inf)
    tree_score_matrix = jnp.einsum('teo,ueo->etu', query_full_rows, tree_key_rows.astype(jnp.float32)) * attention_score_scale
    tree_score_matrix = jnp.where(ancestry[None] > 0.5, tree_score_matrix, -jnp.inf)
    largest = jnp.maximum(lax.optimization_barrier(jnp.max(cache_scores, axis=-1, keepdims=True)), lax.optimization_barrier(jnp.max(tree_score_matrix, axis=-1, keepdims=True)))
    cache_exp = jnp.exp(cache_scores - largest)
    tree_exp = jnp.exp(tree_score_matrix - largest)
    totals = lax.optimization_barrier(jnp.sum(cache_exp, axis=-1, keepdims=True)) + lax.optimization_barrier(jnp.sum(tree_exp, axis=-1, keepdims=True))
    cache_weights = (cache_exp / totals).astype(jnp.bfloat16)
    tree_weight_matrix = (tree_exp / totals).astype(jnp.bfloat16)
    final_output = jnp.einsum('hnc,chd->nhd', cache_weights.astype(jnp.float32), values_cache.astype(jnp.float32))
    final_output = final_output + jnp.einsum('ilf,fiz->liz', tree_weight_matrix.astype(jnp.float32), tree_value_rows.astype(jnp.float32))
    return final_output.astype(jnp.bfloat16)

def reference(stream, row_tree_nodes, input_norm_gain, query_key_value_weight, adapter_down_weight, adapter_up_weight, key_value_cache, cache_length, parents, accepted, output_weight):
    complete_width = HEAD_COUNT * HEAD_SIZE
    wide_rows = stream.astype(jnp.float32)
    inverse_rms = lax.rsqrt(lax.optimization_barrier(jnp.mean(wide_rows * wide_rows, axis=1, keepdims=True)) + 1e-05)
    normalized_input = (wide_rows * inverse_rms * input_norm_gain.astype(jnp.float32)).astype(jnp.bfloat16)
    reduced_rank_rows = jnp.dot(normalized_input, adapter_down_weight, preferred_element_type=jnp.float32).astype(jnp.bfloat16)
    query_key_value_sum = jnp.dot(normalized_input, query_key_value_weight.reshape(INPUT_WIDTH, 3 * complete_width), preferred_element_type=jnp.float32)
    query_key_value_sum = query_key_value_sum + jnp.dot(reduced_rank_rows, adapter_up_weight.reshape(ADAPTER_RANK, 3 * complete_width), preferred_element_type=jnp.float32)
    qkv = query_key_value_sum.astype(jnp.bfloat16)
    node_to_row = jnp.argsort(row_tree_nodes)
    node_qkv = qkv[node_to_row].reshape(REQ, NODES, 3, HEAD_COUNT, HEAD_SIZE)
    ancestry = ancestors_of(parents)
    keys_cache = key_value_cache[0].reshape(REQ, CACHE, HEAD_COUNT, HEAD_SIZE)
    values_cache = key_value_cache[1].reshape(REQ, CACHE, HEAD_COUNT, HEAD_SIZE)
    attention = lax.map(attend_one, (node_qkv[:, :, 0], node_qkv[:, :, 1], node_qkv[:, :, 2], keys_cache, values_cache, cache_length, ancestry))
    head_rows = attention.reshape(TOKENS, complete_width)[row_tree_nodes]
    attended = jnp.dot(head_rows, output_weight, preferred_element_type=jnp.float32).astype(jnp.bfloat16)
    node_table = node_qkv.reshape(REQ, NODES, 3, complete_width)
    chosen = jnp.take_along_axis(node_table, accepted[:, :, None, None], axis=1)
    accepted_kv = jnp.stack([chosen[:, :, 1], chosen[:, :, 2]])
    return (attended, accepted_kv)
```

```python
import functools

import jax
import jax.numpy as jnp
from jax import lax
from jax.experimental import pallas as pl
from jax.experimental.pallas import tpu as pltpu
from jax.sharding import PartitionSpec as P

HEAD_SIZE = 224
NODES = 64
LANES = 128
F32 = jnp.float32
BF16 = jnp.bfloat16
VMEM_BYTES = 50 * 2**20


def dot(a, b, dims=((1,), (0,))):
    return lax.dot_general(a, b, (dims, ((), ())), preferred_element_type=F32)


def whole(shape):
    return pl.BlockSpec(shape, lambda *_: (0,) * len(shape))


def params():
    return pltpu.CompilerParams(vmem_limit_bytes=VMEM_BYTES)


def row_to_column(row):
    size = row.shape[1]
    eye = lax.broadcasted_iota(jnp.int32, (size, size), 0) == lax.broadcasted_iota(
        jnp.int32, (size, size), 1
    )
    return jnp.sum(jnp.where(eye, row, 0), axis=1, keepdims=True)


def rank_in_plane(row):
    before = row_to_column(row) < row
    return jnp.sum(before.astype(jnp.int32), axis=0, keepdims=True)


def norm_kernel(slots, rank_rows, ids_ref, stream_ref, gain_ref, down_ref, first_ref, second_ref,
                place_ref, normed):
    me = lax.axis_index("head")
    plane = lax.axis_index("tok")
    rows, width = stream_ref.shape
    step = 32
    gain = gain_ref[...].astype(F32)

    def chunk(i, carry):
        at = pl.ds(pl.multiple_of(i * step, step), step)
        wide = stream_ref[at, :].astype(F32)
        rstd = lax.rsqrt(jnp.sum(wide * wide, axis=1, keepdims=True) / width + 1e-05)
        normed[at, :] = (wide * rstd * gain).astype(BF16)
        return carry

    lax.fori_loop(0, rows // step, chunk, 0)
    low = dot(normed[...], down_ref[...]).astype(BF16)
    ranks = low.shape[1]
    pick = lax.broadcasted_iota(jnp.int32, (ranks, LANES), 0) == (
        lax.broadcasted_iota(jnp.int32, (ranks, LANES), 1) + me * rank_rows
    )
    pick &= lax.broadcasted_iota(jnp.int32, (ranks, LANES), 1) < rank_rows
    low = dot(low, pick.astype(BF16)).astype(BF16)
    ids = ids_ref[pl.ds(plane, 1), :]
    rank = rank_in_plane(ids)
    owner = ids // (2 * NODES)
    second = (ids // NODES) % 2
    apart = owner ^ me
    even = (owner & 1) == 0
    bit_x = (apart >> 1) & 1
    bit_y = (apart >> 2) & 1
    order = (apart & 1) * 4 + jnp.where(even, bit_x * 2 + bit_y, bit_y * 2 + bit_x)
    position = second * (rows // 2) + order * slots + rank % slots
    place = (lax.broadcasted_iota(jnp.int32, (rows, rows), 0) == position).astype(BF16)
    place_ref[...] = place
    columns = first_ref.shape[1] - LANES
    block = normed[:, pl.ds(pl.multiple_of(me * columns, LANES), columns)]
    sorted_block = dot(place, block).astype(BF16)
    sorted_low = dot(place, low).astype(BF16)
    half = rows // 2
    first_ref[:, :columns] = sorted_block[:half]
    second_ref[:, :columns] = sorted_block[half:]
    first_ref[:, columns:] = sorted_low[:half]
    second_ref[:, columns:] = sorted_low[half:]


def prep_kernel(slots, ids_ref, parents_ref, accepted_ref, mask_ref, chosen_ref):
    me = lax.axis_index("head")
    plane = lax.axis_index("tok")
    planes, rows = ids_ref.shape
    for j in range(2):
        nodes = []
        for k in range(planes):
            ids = ids_ref[pl.ds(plane ^ k, 1), :]
            rank = rank_in_plane(ids)
            spot = lax.broadcasted_iota(jnp.int32, (slots, rows), 0) + (me * 2 + j) * slots
            nodes.append(
                jnp.sum(jnp.where(rank == spot, ids, 0), axis=1, keepdims=True)
                - (me * 2 + j) * NODES
            )
        nodes = jnp.concatenate(nodes, axis=0)
        lanes = lax.broadcasted_iota(jnp.int32, (NODES, NODES), 1)
        rows_of = lax.broadcasted_iota(jnp.int32, (NODES, NODES), 0)
        named = (nodes == lanes).astype(BF16)
        parent = row_to_column(parents_ref[j : j + 1, :])
        reach = ((parent == lanes) | (rows_of == lanes)).astype(BF16)
        for _ in range((NODES - 1).bit_length()):
            reach = jnp.minimum(dot(reach, reach), 1.0).astype(BF16)
        mask_ref[j] = dot(dot(named, reach).astype(BF16), named, ((1,), (1,)))
        accepted = row_to_column(accepted_ref[j : j + 1, :])
        depth = accepted.shape[0]
        wanted = (accepted == lax.broadcasted_iota(jnp.int32, (depth, NODES), 1)).astype(BF16)
        chosen_ref[j] = dot(wanted, named, ((1,), (1,)))


def project_kernel(pieces, groups, rank_rows, *refs):
    lhs_refs = refs[:pieces]
    weight_ref, up_ref, keep_ref, send_ref = refs[pieces:]
    columns = weight_ref.shape[0]
    at = 0
    for lhs_ref in lhs_refs:
        rows = lhs_ref.shape[0] // groups
        for g in range(groups):
            lhs = lhs_ref[g * rows : (g + 1) * rows, :]
            total = dot(lhs[:, :columns], weight_ref[...])
            total += dot(lhs[:, columns : columns + rank_rows], up_ref[...])
            keep_ref[at : at + rows // 2, :] = total[: rows // 2]
            send_ref[at : at + rows // 2, :] = total[rows // 2 :].astype(BF16)
            at += rows // 2


def project(pieces, groups, weight, up):
    parts, columns, width = weight.shape
    rank_rows = up.shape[1]
    tile = width // 2
    rows = sum(piece.shape[0] for piece in pieces) // 2
    return pl.pallas_call(
        functools.partial(project_kernel, len(pieces), groups, rank_rows),
        grid=(parts, 2),
        in_specs=[whole(piece.shape) for piece in pieces]
        + [
            pl.BlockSpec((None, columns, tile), lambda p, c: (p, 0, c)),
            pl.BlockSpec((None, rank_rows, tile), lambda p, c: (p, 0, c)),
        ],
        out_specs=[
            pl.BlockSpec((rows, tile), lambda p, c: (0, p * 2 + c)),
            pl.BlockSpec((rows, tile), lambda p, c: (0, p * 2 + c)),
        ],
        out_shape=[
            jax.ShapeDtypeStruct((rows, parts * width), F32),
            jax.ShapeDtypeStruct((rows, parts * width), BF16),
        ],
        compiler_params=params(),
        cost_estimate=pl.CostEstimate(
            flops=4 * rows * (columns + 128) * parts * width,
            bytes_accessed=2 * columns * parts * width + 6 * rows * parts * width,
            transcendentals=0,
        ),
    )(*pieces, weight, up)


def attend_kernel(span, heads, length_ref, query_ref, key_ref, value_ref, mask_ref, chosen_ref,
                  cache_key_ref, cache_value_ref, out_ref, kept_ref, spread, top, total, acc):
    block = pl.program_id(1)
    width = query_ref.shape[1]
    scale = HEAD_SIZE ** (-0.5)
    head_of_lane = lax.broadcasted_iota(jnp.int32, (1, width), 1) // HEAD_SIZE
    length = length_ref[0]

    def fold(scores, values, first):
        peak = jnp.max(scores, axis=1, keepdims=True)
        if not first:
            before = top[...]
            peak = jnp.maximum(before, peak)
        weights = jnp.exp(scores - peak)
        gained = jnp.sum(weights, axis=1, keepdims=True)
        part = dot(weights.astype(BF16), values)
        if first:
            total[...] = gained
            acc[...] = part
        else:
            shrink = jnp.exp(before - peak)
            total[...] = total[...] * shrink + gained
            acc[...] = acc[...] * shrink + part
        top[...] = peak

    @pl.when(block == 0)
    def start():
        query = query_ref[...]
        for h in range(heads):
            spread[h * NODES : (h + 1) * NODES, :] = jnp.where(head_of_lane == h, query, 0)
        scores = dot(spread[...], key_ref[...], ((1,), (1,))) * scale
        allowed = jnp.concatenate([mask_ref[...]] * heads, axis=0) > 0.5
        fold(jnp.where(allowed, scores, -1e30), value_ref[...], True)
        pick = chosen_ref[...].astype(BF16)
        kept_ref[0] = dot(pick, key_ref[...]).astype(BF16)
        kept_ref[1] = dot(pick, value_ref[...]).astype(BF16)

    @pl.when(block * span < length)
    def cached():
        scores = dot(spread[...], cache_key_ref[...], ((1,), (1,))) * scale
        spot = lax.broadcasted_iota(jnp.int32, (1, span), 1) + block * span
        fold(jnp.where(spot < length, scores, -1e30), cache_value_ref[...], False)

    @pl.when(block == pl.num_programs(1) - 1)
    def finish():
        share = acc[...] / total[...]
        out = jnp.zeros((NODES, width), F32)
        for h in range(heads):
            out = jnp.where(head_of_lane == h, share[h * NODES : (h + 1) * NODES, :], out)
        out_ref[...] = out.astype(BF16)


def attend(j, lengths, triple, masks, chosen, cache):
    cache_span, width = cache.shape[2:]
    tile = 4 * HEAD_SIZE
    groups = width // tile
    span = min(1024, cache_span)
    depth = chosen.shape[1]

    def cached(part):
        def index(g, b, length):
            return (part, j, jnp.minimum(b, (length[0] - 1) // span), g)

        return pl.BlockSpec((None, None, span, tile), index)

    def column(part):
        return pl.BlockSpec((NODES, tile), lambda g, b, length: (0, part * groups + g))

    return pl.pallas_call(
        functools.partial(attend_kernel, span, 4),
        grid_spec=pltpu.PrefetchScalarGridSpec(
            num_scalar_prefetch=1,
            grid=(groups, cache_span // span),
            in_specs=[
                column(0),
                column(1),
                column(2),
                pl.BlockSpec((None, NODES, NODES), lambda g, b, length: (j, 0, 0)),
                pl.BlockSpec((None, depth, NODES), lambda g, b, length: (j, 0, 0)),
                cached(0),
                cached(1),
            ],
            out_specs=[
                pl.BlockSpec((NODES, tile), lambda g, b, length: (0, g)),
                pl.BlockSpec((2, depth, tile), lambda g, b, length: (0, 0, g)),
            ],
            scratch_shapes=[
                pltpu.VMEM((4 * NODES, tile), BF16),
                pltpu.VMEM((4 * NODES, 1), F32),
                pltpu.VMEM((4 * NODES, 1), F32),
                pltpu.VMEM((4 * NODES, tile), F32),
            ],
        ),
        out_shape=[
            jax.ShapeDtypeStruct((NODES, width), BF16),
            jax.ShapeDtypeStruct((2, depth, width), BF16),
        ],
        compiler_params=params(),
        cost_estimate=pl.CostEstimate(
            flops=16 * NODES * cache_span * width,
            bytes_accessed=4 * cache_span * width,
            transcendentals=NODES * cache_span * 4 * groups,
        ),
    )(lengths[j : j + 1], triple, triple, triple, masks, chosen, cache, cache)


def lift_kernel(rows_ref, weight_ref, out_ref):
    rows = rows_ref[...].reshape(-1, rows_ref.shape[-1])
    out_ref[...] = dot(weight_ref[...], rows, ((1,), (1,)))


def lift(rows, weight):
    owners, planes, slots, width = rows.shape
    wide = weight.shape[0]
    return pl.pallas_call(
        lift_kernel,
        grid=(planes,),
        in_specs=[
            pl.BlockSpec((owners, None, slots, width), lambda k: (0, k, 0, 0)),
            whole(weight.shape),
        ],
        out_specs=pl.BlockSpec((None, wide, owners * slots), lambda k: (k, 0, 0)),
        out_shape=jax.ShapeDtypeStruct((planes, wide, owners * slots), F32),
        compiler_params=params(),
        cost_estimate=pl.CostEstimate(
            flops=2 * owners * planes * slots * width * wide,
            bytes_accessed=2 * rows.size + 2 * weight.size,
            transcendentals=0,
        ),
    )(rows, weight)


def final_kernel(pieces, place_ref, *refs):
    own = refs[:2]
    others = refs[2:-1]
    out_ref = refs[-1]
    sums = []
    for j in range(2):
        total = own[j][...]
        for piece in others[j * pieces : (j + 1) * pieces]:
            total = total + piece[...].astype(F32)
        sums.append(total.astype(BF16))
    out_ref[...] = dot(jnp.concatenate(sums, axis=1), place_ref[...]).astype(BF16)


def on_device(
    stream,
    row_tree_nodes,
    input_norm_gain,
    query_key_value_weight,
    adapter_down_weight,
    adapter_up_weight,
    key_value_cache,
    cache_length,
    parents,
    accepted,
    output_weight,
):
    rows, width_in = stream.shape
    planes = row_tree_nodes.shape[0] // rows
    owners = width_in // query_key_value_weight.shape[0]
    slots = rows // (2 * owners)
    columns = query_key_value_weight.shape[0]
    width = query_key_value_weight.shape[2]
    rank_rows = adapter_up_weight.shape[0]
    weight = jnp.swapaxes(query_key_value_weight, 0, 1)
    up = jnp.swapaxes(adapter_up_weight, 0, 1)
    down = jnp.swapaxes(output_weight, 0, 1)
    ids = row_tree_nodes.reshape(planes, rows)

    def first_mask(h):
        return 2 if h % 2 == 0 else 4

    core_pairs = [(h, h ^ 1) for h in range(owners)]
    first_pairs = [(h, h ^ first_mask(h)) for h in range(owners)]
    second_pairs = [(h, h ^ (6 - first_mask(h))) for h in range(owners)]

    def across(array, k):
        return lax.ppermute(array, "tok", [(z, z ^ k) for z in range(planes)])

    feature = jax.ShapeDtypeStruct((rows // 2, columns + LANES), BF16)
    first, second, place = pl.pallas_call(
        functools.partial(norm_kernel, slots, rank_rows),
        out_shape=[feature, feature, jax.ShapeDtypeStruct((rows, rows), BF16)],
        scratch_shapes=[pltpu.VMEM((rows, width_in), BF16)],
        compiler_params=params(),
    )(ids, stream, input_norm_gain.reshape(1, -1), adapter_down_weight)
    near = [first, second]
    far = [[across(near[j], k) for k in range(1, planes)] for j in range(2)]
    depth = accepted.shape[1]
    masks, chosen = pl.pallas_call(
        functools.partial(prep_kernel, slots),
        out_shape=[
            jax.ShapeDtypeStruct((2, NODES, NODES), F32),
            jax.ShapeDtypeStruct((2, depth, NODES), F32),
        ],
        compiler_params=params(),
    )(ids, parents, accepted)

    def scatter(keep, send, batch):
        keep = keep.reshape(batch, 4 * slots, -1)
        send = send.reshape(batch, 4 * slots, -1)
        for pairs, left in ((core_pairs, 4), (first_pairs, 2), (second_pairs, 1)):
            got = lax.ppermute(send, "head", pairs)
            added = keep + got.astype(F32)
            if left == 1:
                return added.astype(BF16)
            cut = left * slots // 2
            send = added[:, cut:].astype(BF16)
            keep = added[:, :cut]

    own = scatter(*project(near, 1, weight, up), 2)
    finished = []
    kept = []
    for j in range(2):
        rest = scatter(*project(far[j], 1, weight, up), planes - 1)
        triple = jnp.concatenate([own[j], rest.reshape(-1, rest.shape[-1])], axis=0)
        gathered, saved = attend(j, cache_length, triple, masks, chosen, key_value_cache)
        kept.append(saved)
        gathered = gathered.reshape(1, planes, slots, width)
        for pairs in (second_pairs, first_pairs, core_pairs):
            gathered = jnp.concatenate([gathered, lax.ppermute(gathered, "head", pairs)], axis=0)
        lifted = lift(gathered, down)
        finished.append(
            (lifted[0], [across(lifted[k].astype(BF16), k) for k in range(1, planes)])
        )
    attended = pl.pallas_call(
        functools.partial(final_kernel, planes - 1),
        out_shape=jax.ShapeDtypeStruct((output_weight.shape[1], rows), BF16),
        compiler_params=params(),
    )(place, finished[0][0], finished[1][0], *finished[0][1], *finished[1][1])
    return jnp.swapaxes(attended, 0, 1), jnp.stack(kept, axis=1)


def ancestors_of(parents):
    parent_links = jax.nn.one_hot(parents, NODES, dtype=jnp.float32)
    identity_matrix = jnp.eye(NODES, dtype=jnp.float32)
    ancestry = jnp.minimum(identity_matrix[None] + parent_links, 1.0)
    for squaring in range(NODES.bit_length()):
        ancestry = jnp.minimum(
            jnp.einsum("rnm,rmk->rnk", ancestry, ancestry, precision=lax.Precision.HIGHEST), 1.0
        )
    return ancestry


def plain_on_device(
    stream,
    row_tree_nodes,
    input_norm_gain,
    query_key_value_weight,
    adapter_down_weight,
    adapter_up_weight,
    key_value_cache,
    cache_length,
    parents,
    accepted,
    output_weight,
):
    owner_index = lax.axis_index("head")
    feature_rows = query_key_value_weight.shape[0]
    device_width = query_key_value_weight.shape[2]
    adapter_rank_rows = adapter_up_weight.shape[0]
    local_heads = device_width // HEAD_SIZE
    request_count = key_value_cache.shape[1]
    cache_span = key_value_cache.shape[2]
    wide_rows = stream.astype(jnp.float32)
    inverse_rms = lax.rsqrt(jnp.mean(wide_rows * wide_rows, axis=1, keepdims=True) + 1e-05)
    normalized_input = (wide_rows * inverse_rms * input_norm_gain.astype(jnp.float32)).astype(
        jnp.bfloat16
    )
    reduced_rank_rows = jnp.dot(
        normalized_input, adapter_down_weight, preferred_element_type=jnp.float32
    ).astype(jnp.bfloat16)
    feature_block = lax.dynamic_slice_in_dim(
        normalized_input, owner_index * feature_rows, feature_rows, 1
    )
    rank_block = lax.dynamic_slice_in_dim(
        reduced_rank_rows, owner_index * adapter_rank_rows, adapter_rank_rows, 1
    )
    gathered_features, gathered_ranks = (
        lax.all_gather(feature_block, "tok", axis=0, tiled=True),
        lax.all_gather(rank_block, "tok", axis=0, tiled=True),
    )
    projection = query_key_value_weight.reshape(feature_rows, 3 * device_width)
    lifting_matrix = adapter_up_weight.reshape(adapter_rank_rows, 3 * device_width)
    node_to_row = jnp.argsort(row_tree_nodes)
    part_sum = jnp.dot(
        gathered_features[node_to_row], projection, preferred_element_type=jnp.float32
    )
    node_rows = lax.psum_scatter(
        part_sum
        + jnp.dot(gathered_ranks[node_to_row], lifting_matrix, preferred_element_type=jnp.float32),
        "head",
        scatter_dimension=0,
        tiled=True,
    ).astype(jnp.bfloat16)
    triple = node_rows.reshape(request_count, NODES, 3, local_heads, HEAD_SIZE)
    queries = triple[:, :, 0]
    tree_key_rows = triple[:, :, 1]
    tree_value_rows = triple[:, :, 2]
    ancestry = ancestors_of(parents)
    attention_score_scale = HEAD_SIZE ** (-0.5)
    tree_score_matrix = (
        jnp.einsum("rnhd,rmhd->rhnm", queries, tree_key_rows, preferred_element_type=jnp.float32)
        * attention_score_scale
    )
    tree_score_matrix = jnp.where(ancestry[:, None] > 0.5, tree_score_matrix, -jnp.inf)
    keys_cache = key_value_cache[0].reshape(request_count, cache_span, local_heads, HEAD_SIZE)
    values_cache = key_value_cache[1].reshape(request_count, cache_span, local_heads, HEAD_SIZE)
    scores = (
        jnp.einsum("rnhd,rchd->rhnc", queries, keys_cache, preferred_element_type=jnp.float32)
        * attention_score_scale
    )
    positions = lax.broadcasted_iota(jnp.int32, (1, 1, 1, cache_span), 3)
    scores = jnp.where(positions < cache_length[:, None, None, None], scores, -jnp.inf)
    tree_top = jnp.max(tree_score_matrix, axis=-1, keepdims=True)
    largest = jnp.maximum(tree_top, jnp.max(scores, axis=-1, keepdims=True))
    cache_exp = jnp.exp(scores - largest)
    tree_exp = jnp.exp(tree_score_matrix - largest)
    totals = jnp.sum(cache_exp, axis=-1, keepdims=True) + jnp.sum(tree_exp, axis=-1, keepdims=True)
    cache_weights = (cache_exp / totals).astype(jnp.bfloat16)
    tree_weight_matrix = (tree_exp / totals).astype(jnp.bfloat16)
    attention = jnp.einsum(
        "rhnc,rchd->rnhd", cache_weights, values_cache, preferred_element_type=jnp.float32
    )
    attention = attention + jnp.einsum(
        "rhnm,rmhd->rnhd", tree_weight_matrix, tree_value_rows, preferred_element_type=jnp.float32
    )
    head_rows = attention.astype(jnp.bfloat16).reshape(request_count * NODES, device_width)
    node_table = node_rows.reshape(request_count, NODES, 3, device_width)
    chosen = jnp.take_along_axis(node_table, accepted[:, :, None, None], axis=1)
    accepted_kv = jnp.stack([chosen[:, :, 1], chosen[:, :, 2]])
    everything = lax.all_gather(head_rows, "head", axis=0, tiled=True)
    attended = lax.psum_scatter(
        jnp.dot(
            everything[row_tree_nodes], output_weight, preferred_element_type=jnp.float32
        ).astype(jnp.bfloat16),
        "tok",
        scatter_dimension=0,
        tiled=True,
    )
    return (attended, accepted_kv)


def solution(mesh):
    placed = (
        P("tok", None),
        P(),
        P(),
        P("head", None, "tok"),
        P(),
        P("head", None, "tok"),
        P(None, "head", None, "tok"),
        P("head"),
        P("head", None),
        P("head", None),
        P("tok", "head"),
    )
    sized = mesh.shape["head"] == 8 and mesh.shape["tok"] == 4
    return jax.shard_map(
        on_device if sized else plain_on_device,
        mesh=mesh,
        in_specs=placed,
        out_specs=(P("tok", "head"), P(None, "head", None, "tok")),
        check_vma=False,
    )
```

```python
import functools

import jax
import jax.numpy as jnp
from jax import lax
from jax.experimental import pallas as pl
from jax.experimental.pallas import tpu as pltpu
from jax.sharding import PartitionSpec as P

HEAD_SIZE = 224
NODES = 64
LANES = 128
F32 = jnp.float32
BF16 = jnp.bfloat16
SMALL = pl.CostEstimate(flops=1, bytes_accessed=1, transcendentals=0)
LARGE = pl.CostEstimate(flops=2 * 10**11, bytes_accessed=1, transcendentals=0)


def dot(a, b, dims=((1,), (0,))):
    return lax.dot_general(a, b, (dims, ((), ())), preferred_element_type=F32)


def whole(shape):
    return pl.BlockSpec(shape, lambda *_: (0,) * len(shape))


def ordered(kernel, after, operands, in_specs, megabytes, cost=SMALL, **options):
    count = len(after)

    def body(*refs):
        kernel(*refs[count:])

    return pl.pallas_call(
        body,
        in_specs=[pl.BlockSpec(memory_space=pl.ANY)] * count + in_specs,
        compiler_params=pltpu.CompilerParams(vmem_limit_bytes=megabytes * 2**20),
        cost_estimate=cost,
        **options,
    )(*after, *operands)


def row_to_column(row):
    size = row.shape[1]
    eye = lax.broadcasted_iota(jnp.int32, (size, size), 0) == lax.broadcasted_iota(
        jnp.int32, (size, size), 1
    )
    return jnp.sum(jnp.where(eye, row, 0), axis=1, keepdims=True)


def rank_in_plane(row):
    before = row_to_column(row) < row
    return jnp.sum(before.astype(jnp.int32), axis=0, keepdims=True)


def plane_row(ids_ref, plane, rows):
    per = rows // LANES
    parts = [ids_ref[pl.ds(plane * per + i, 1), :] for i in range(per)]
    return jnp.concatenate(parts, axis=1)


CHUNK = 32


def norm_kernel(slots, rank_rows, ids_ref, stream_hbm, gain_ref, down_hbm, first_ref, second_ref,
                place_ref, normed, held, down_ref, arrived, down_arrived):
    me = lax.axis_index("head")
    plane = lax.axis_index("tok")
    rows, width = held.shape
    copies = [
        pltpu.make_async_copy(
            stream_hbm.at[pl.ds(i * CHUNK, CHUNK), :],
            held.at[pl.ds(i * CHUNK, CHUNK), :],
            arrived.at[i],
        )
        for i in range(rows // CHUNK)
    ]
    for copy in copies:
        copy.start()
    down_copy = pltpu.make_async_copy(down_hbm, down_ref, down_arrived)
    down_copy.start()
    gains = gain_ref[...].astype(F32)
    gain = jnp.concatenate([gains[i : i + 1] for i in range(width // LANES)], axis=1)

    def norm(i, carry):
        at = pl.ds(pl.multiple_of(i * CHUNK, CHUNK), CHUNK)
        pltpu.make_async_copy(stream_hbm.at[at, :], held.at[at, :], arrived.at[i]).wait()
        wide = held[at, :].astype(F32)
        rstd = lax.rsqrt(jnp.sum(wide * wide, axis=1, keepdims=True) / width + 1e-05)
        normed[at, :] = (wide * rstd * gain).astype(BF16)
        return carry

    lax.fori_loop(0, rows // CHUNK, norm, 0)
    down_copy.wait()
    low = dot(normed[...], down_ref[...]).astype(BF16)
    ranks = low.shape[1]
    lane = lax.broadcasted_iota(jnp.int32, (ranks, LANES), 1)
    wanted = jnp.where(lane < rank_rows, me * rank_rows + lane, (me ^ 1) * rank_rows + lane - rank_rows)
    pick = lax.broadcasted_iota(jnp.int32, (ranks, LANES), 0) == wanted
    pick &= lane < 2 * rank_rows
    low = dot(low, pick.astype(BF16)).astype(BF16)
    ids = plane_row(ids_ref, plane, rows)
    rank = rank_in_plane(ids)
    owner = ids // (2 * NODES)
    second = (ids // NODES) % 2
    apart = owner ^ me
    even = (owner & 1) == 0
    bit_x = (apart >> 1) & 1
    bit_y = (apart >> 2) & 1
    order = (apart & 1) * 4 + jnp.where(even, bit_x * 2 + bit_y, bit_y * 2 + bit_x)
    half = rows // 2
    position = second * half + order * slots + rank % slots
    place_ref[...] = (
        lax.broadcasted_iota(jnp.int32, (rows, rows), 0) == position
    ).astype(BF16)
    quarter = half // 2
    position = jnp.where(order < 4, second * quarter + order * slots + rank % slots, -1)
    place = (lax.broadcasted_iota(jnp.int32, (half, rows), 0) == position).astype(BF16)
    columns = (first_ref.shape[1] - LANES) // 2
    for i, owner_of in enumerate((me, me ^ 1)):
        block = normed[:, pl.ds(pl.multiple_of(owner_of * columns, LANES), columns)]
        sorted_block = dot(place, block).astype(BF16)
        first_ref[:, i * columns : (i + 1) * columns] = sorted_block[:quarter]
        second_ref[:, i * columns : (i + 1) * columns] = sorted_block[quarter:]
    sorted_low = dot(place, low).astype(BF16)
    first_ref[:, 2 * columns :] = sorted_low[:quarter]
    second_ref[:, 2 * columns :] = sorted_low[quarter:]


def prep_kernel(slots, planes, rows, ids_ref, parents_ref, accepted_ref, mask_ref, chosen_ref):
    me = lax.axis_index("head")
    plane = lax.axis_index("tok")
    for j in range(2):
        nodes = []
        for k in range(planes):
            ids = plane_row(ids_ref, plane ^ k, rows)
            rank = rank_in_plane(ids)
            spot = lax.broadcasted_iota(jnp.int32, (slots, rows), 0) + (me * 2 + j) * slots
            nodes.append(
                jnp.sum(jnp.where(rank == spot, ids, 0), axis=1, keepdims=True)
                - (me * 2 + j) * NODES
            )
        nodes = jnp.concatenate(nodes, axis=0)
        lanes = lax.broadcasted_iota(jnp.int32, (NODES, NODES), 1)
        rows_of = lax.broadcasted_iota(jnp.int32, (NODES, NODES), 0)
        named = (nodes == lanes).astype(BF16)
        parent = row_to_column(parents_ref[j : j + 1, :])
        reach = ((parent == lanes) | (rows_of == lanes)).astype(BF16)
        for _ in range((NODES - 1).bit_length()):
            reach = jnp.minimum(dot(reach, reach), 1.0).astype(BF16)
        mask_ref[j] = dot(dot(named, reach).astype(BF16), named, ((1,), (1,)))
        accepted = row_to_column(accepted_ref[j : j + 1, :])
        depth = accepted.shape[0]
        wanted = (accepted == lax.broadcasted_iota(jnp.int32, (depth, NODES), 1)).astype(BF16)
        chosen_ref[j] = dot(wanted, named, ((1,), (1,)))


def tiles_of(width):
    first = (width // 512 + 1) * 256 if width % 512 else width // 2
    return [(0, first), (first, width - first)]


def project_kernel(pieces, *refs):
    lhs_refs = refs[:pieces]
    weight_refs = refs[pieces : pieces + 2]
    up_refs = refs[pieces + 2 : pieces + 4]
    keep_hbm, send_hbm = refs[pieces + 4 : pieces + 6]
    lhs, held, keep, send, arrived, left = refs[-6:]
    parts, columns, width = weight_refs[0].shape
    deep = held.shape[1]
    half = lhs.shape[0] // 2
    rank_rows = up_refs[0].shape[1]
    steps = [(p, start, size) for p in range(parts) for start, size in tiles_of(width)]

    def inward(i, side):
        p, start, size = steps[i]
        return pltpu.make_async_copy(
            weight_refs[side].at[p, :, pl.ds(start, size)],
            held.at[p, pl.ds(side * columns, columns), pl.ds(start, size)],
            arrived.at[i, side],
        )

    for i in range(len(steps)):
        for side in range(2):
            inward(i, side).start()
    at = 0
    for lhs_ref in lhs_refs:
        rows = lhs_ref.shape[0] // 2
        lhs[at : at + rows, :] = lhs_ref[:rows, :]
        lhs[half + at : half + at + rows, :] = lhs_ref[rows:, :]
        at += rows
    for p in range(parts):
        low = 2 * columns
        for side in range(2):
            held[p, low : low + rank_rows, :] = up_refs[side][p]
            low += rank_rows
        held[p, low:, :] = jnp.zeros((deep - low, width), BF16)
    outward = []
    for i, (p, start, size) in enumerate(steps):
        for side in range(2):
            inward(i, side).wait()
        lanes = slice(p * width + start, p * width + start + size)
        total = dot(lhs[...], held[p, :, start : start + size])
        keep[:, lanes] = total[:half]
        send[:, lanes] = total[half:].astype(BF16)
        for j, (source, target) in enumerate(((keep, keep_hbm), (send, send_hbm))):
            copy = pltpu.make_async_copy(source.at[:, lanes], target.at[:, lanes], left.at[i, j])
            copy.start()
            outward.append(copy)
    for copy in outward:
        copy.wait()


def project(pieces, weights, ups, after=()):
    parts, columns, width = weights[0].shape
    steps = parts * len(tiles_of(width))
    rows = sum(piece.shape[0] for piece in pieces) // 2
    deep = pieces[0].shape[1]
    far = pl.BlockSpec(memory_space=pltpu.HBM)
    return ordered(
        functools.partial(project_kernel, len(pieces)),
        after,
        (*pieces, *weights, *ups),
        [whole(piece.shape) for piece in pieces] + [far] * 2 + [whole(ups[0].shape)] * 2,
        58,
        LARGE,
        out_specs=[far] * 2,
        out_shape=[
            jax.ShapeDtypeStruct((rows, parts * width), F32),
            jax.ShapeDtypeStruct((rows, parts * width), BF16),
        ],
        scratch_shapes=[
            pltpu.VMEM((2 * rows, deep), BF16),
            pltpu.VMEM((parts, deep, width), BF16),
            pltpu.VMEM((rows, parts * width), F32),
            pltpu.VMEM((rows, parts * width), BF16),
            pltpu.SemaphoreType.DMA((steps, 2)),
            pltpu.SemaphoreType.DMA((steps, 2)),
        ],
    )


def halve_kernel(keep_ref, got_ref, kept_ref, send_ref):
    added = keep_ref[...] + got_ref[...].astype(F32)
    half = added.shape[1] // 2
    kept_ref[...] = added[:, :half]
    send_ref[...] = added[:, half:].astype(BF16)


def halve(keep, got, parts, after=()):
    batch, rows, wide = keep.shape
    tile = wide // parts
    half = rows // 2

    def block(rows):
        return pl.BlockSpec((batch, rows, tile), lambda c: (0, 0, c))

    return ordered(
        halve_kernel,
        after,
        (keep, got),
        [block(rows)] * 2,
        16,
        grid=(parts,),
        out_specs=[block(half)] * 2,
        out_shape=[
            jax.ShapeDtypeStruct((batch, half, wide), F32),
            jax.ShapeDtypeStruct((batch, half, wide), BF16),
        ],
    )


def join_kernel(own_keep_ref, own_got_ref, keep_ref, got_ref, out_ref):
    slots = own_keep_ref.shape[0]
    out_ref[:slots] = (own_keep_ref[...] + own_got_ref[...].astype(F32)).astype(BF16)
    for k in range(keep_ref.shape[0]):
        out_ref[(k + 1) * slots : (k + 2) * slots] = (
            keep_ref[k] + got_ref[k].astype(F32)
        ).astype(BF16)


def join(j, own, rest, parts, after=()):
    batch, slots, wide = rest[0].shape
    tile = wide // parts
    near = pl.BlockSpec((None, slots, tile), lambda c: (j, 0, c))
    far = pl.BlockSpec((batch, slots, tile), lambda c: (0, 0, c))
    return ordered(
        join_kernel,
        after,
        (*own, *rest),
        [near, near, far, far],
        16,
        grid=(parts,),
        out_specs=pl.BlockSpec(((batch + 1) * slots, tile), lambda c: (0, c)),
        out_shape=jax.ShapeDtypeStruct(((batch + 1) * slots, wide), BF16),
    )


HEADS = 4
LOG2E = 1.4426950408889634


def attend_kernel(j, span, groups, length_ref, triple_ref, mask_ref, chosen_ref, cache_ref,
                  out_ref, kept_ref, spread, top, total, acc, held, arrived):
    chunks = held.shape[1]
    tile = spread.shape[2]
    width = groups * tile
    length = length_ref[j]
    scale = HEAD_SIZE ** (-0.5) * LOG2E

    def copy(part, c):
        return pltpu.make_async_copy(
            cache_ref.at[part, j, pl.ds(c * span, span), :], held.at[part, c], arrived.at[part, c]
        )

    for c in range(chunks):
        @pl.when(c * span < length)
        def fetch():
            copy(0, c).start()
            copy(1, c).start()

    head_of_lane = lax.broadcasted_iota(jnp.int32, (1, tile), 1) // HEAD_SIZE

    def fold(g, scores, values, first):
        peak = jnp.max(scores, axis=1, keepdims=True)
        if not first:
            before = top[g]
            peak = jnp.maximum(before, peak)
        weights = jnp.exp2(scores - peak)
        gained = jnp.sum(weights, axis=1, keepdims=True)
        part = dot(weights.astype(BF16), values)
        if first:
            total[g] = gained
            acc[g] = part
        else:
            shrink = jnp.exp2(before - peak)
            total[g] = total[g] * shrink + gained
            acc[g] = acc[g] * shrink + part
        top[g] = peak

    allowed = jnp.concatenate([mask_ref[j]] * HEADS, axis=0) > 0.5
    pick = chosen_ref[j].astype(BF16)
    for g in range(groups):
        lanes = slice(g * tile, (g + 1) * tile)
        query = triple_ref[:, lanes]
        keys = triple_ref[:, width + g * tile : width + (g + 1) * tile]
        values = triple_ref[:, 2 * width + g * tile : 2 * width + (g + 1) * tile]
        for h in range(HEADS):
            spread[g, h * NODES : (h + 1) * NODES, :] = jnp.where(head_of_lane == h, query, 0)
        scores = dot(spread[g], keys, ((1,), (1,))) * scale
        fold(g, jnp.where(allowed, scores, -1e30), values, True)
        kept_ref[0, :, lanes] = dot(pick, keys).astype(BF16)
        kept_ref[1, :, lanes] = dot(pick, values).astype(BF16)

    for c in range(chunks):
        @pl.when(c * span < length)
        def cached():
            copy(0, c).wait()
            copy(1, c).wait()
            spot = lax.broadcasted_iota(jnp.int32, (1, span), 1) + c * span
            bias = jnp.where(spot < length, 0.0, -1e30)
            for g in range(groups):
                lanes = slice(g * tile, (g + 1) * tile)
                scores = dot(spread[g], held[0, c, :, lanes], ((1,), (1,)))
                fold(g, scores * scale + bias, held[1, c, :, lanes], False)

    for g in range(groups):
        share = acc[g] / total[g]
        out = jnp.zeros((NODES, tile), F32)
        for h in range(HEADS):
            out = jnp.where(head_of_lane == h, share[h * NODES : (h + 1) * NODES, :], out)
        out_ref[:, g * tile : (g + 1) * tile] = out.astype(BF16)


def attend(j, lengths, triple, masks, chosen, cache, after=()):
    cache_span, width = cache.shape[2:]
    tile = HEADS * HEAD_SIZE
    groups = width // tile
    span = min(512, cache_span)
    chunks = cache_span // span
    depth = chosen.shape[1]
    return ordered(
        functools.partial(attend_kernel, j, span, groups),
        after,
        (lengths, triple, masks, chosen, cache),
        [
            pl.BlockSpec(memory_space=pltpu.SMEM),
            whole(triple.shape),
            whole(masks.shape),
            whole(chosen.shape),
            pl.BlockSpec(memory_space=pltpu.HBM),
        ],
        32,
        out_specs=[whole((NODES, width)), whole((2, depth, width))],
        out_shape=[
            jax.ShapeDtypeStruct((NODES, width), BF16),
            jax.ShapeDtypeStruct((2, depth, width), BF16),
        ],
        scratch_shapes=[
            pltpu.VMEM((groups, HEADS * NODES, tile), BF16),
            pltpu.VMEM((groups, HEADS * NODES, 1), F32),
            pltpu.VMEM((groups, HEADS * NODES, 1), F32),
            pltpu.VMEM((groups, HEADS * NODES, tile), F32),
            pltpu.VMEM((2, chunks, span, width), BF16),
            pltpu.SemaphoreType.DMA((2, chunks)),
        ],
    )


def pack_kernel(*refs):
    rows = refs[0].shape[0]
    for i, ref in enumerate(refs[:-1]):
        refs[-1][i * rows : (i + 1) * rows, :] = ref[...]


def pack(pieces, after=()):
    rows, width = pieces[0].shape
    return ordered(
        pack_kernel,
        after,
        pieces,
        [whole((rows, width))] * len(pieces),
        16,
        out_shape=jax.ShapeDtypeStruct((rows * len(pieces), width), BF16),
    )


def lift_kernel(planes, slots, *refs):
    pieces = refs[:-4]
    weight_ref, own_ref, other_ref, rows = refs[-4:]
    share = rows.shape[0] // planes
    for k in range(planes):
        at = k * share
        for piece in pieces:
            for q in range(piece.shape[0] // (planes * slots)):
                rows[at : at + slots, :] = piece[
                    (q * planes + k) * slots : (q * planes + k + 1) * slots, :
                ]
                at += slots
    lifted = dot(weight_ref[...], rows[...], ((1,), (1,)))
    for k in range(planes):
        piece = lifted[:, k * share : (k + 1) * share]
        if k % 2 == 0:
            own_ref[k // 2] = piece
        else:
            other_ref[k // 2] = piece.astype(BF16)


def lift(pieces, planes, slots, weight, after=()):
    wide, width = weight.shape
    rows = sum(piece.shape[0] for piece in pieces)
    return ordered(
        functools.partial(lift_kernel, planes, slots),
        after,
        (*pieces, weight),
        [whole(piece.shape) for piece in pieces] + [whole(weight.shape)],
        20,
        out_shape=[
            jax.ShapeDtypeStruct((planes // 2, wide, rows // planes), F32),
            jax.ShapeDtypeStruct((planes // 2, wide, rows // planes), BF16),
        ],
        scratch_shapes=[pltpu.VMEM((rows, width), BF16)],
    )


def settle_kernel(own_ref, got_ref, kept_ref, send_ref, *_):
    kept_ref[...] = own_ref[0] + got_ref[0].astype(F32)
    send_ref[...] = (own_ref[1] + got_ref[1].astype(F32)).astype(BF16)


def settle(own, got, passed=()):
    shape = own.shape[1:]
    return ordered(
        settle_kernel,
        passed,
        (own, got),
        [whole(own.shape)] * 2,
        16,
        out_specs=[whole(shape)] * 2 + [pl.BlockSpec(memory_space=pl.ANY)] * len(passed),
        out_shape=[jax.ShapeDtypeStruct(shape, F32), jax.ShapeDtypeStruct(shape, BF16)]
        + [jax.ShapeDtypeStruct(array.shape, array.dtype) for array in passed],
        input_output_aliases={i: 2 + i for i in range(len(passed))},
    )


def final_kernel(place_ref, *refs):
    sums = [
        (refs[2 * j][...] + refs[2 * j + 1][...].astype(F32)).astype(BF16) for j in range(2)
    ]
    refs[-1][...] = dot(jnp.concatenate(sums, axis=1), place_ref[...]).astype(BF16)


def on_device(
    stream,
    row_tree_nodes,
    input_norm_gain,
    query_key_value_weight,
    adapter_down_weight,
    adapter_up_weight,
    key_value_cache,
    cache_length,
    parents,
    accepted,
    output_weight,
):
    rows, width_in = stream.shape
    planes = row_tree_nodes.shape[0] // rows
    owners = width_in // query_key_value_weight.shape[0]
    slots = rows // (2 * owners)
    columns = query_key_value_weight.shape[0]
    width = query_key_value_weight.shape[2]
    rank_rows = adapter_up_weight.shape[0]
    weight = jnp.swapaxes(query_key_value_weight, 0, 1)
    up = jnp.swapaxes(adapter_up_weight, 0, 1)
    down = jnp.swapaxes(output_weight, 0, 1)
    ids = row_tree_nodes.reshape(-1, LANES)

    def first_mask(h):
        return 2 if h % 2 == 0 else 4

    core_pairs = [(h, h ^ 1) for h in range(owners)]
    first_pairs = [(h, h ^ first_mask(h)) for h in range(owners)]
    second_pairs = [(h, h ^ (6 - first_mask(h))) for h in range(owners)]

    def across(array, k):
        return lax.ppermute(array, "tok", [(z, z ^ k) for z in range(planes)])

    weights = (weight, lax.ppermute(weight, "head", core_pairs))
    ups = (up, lax.ppermute(up, "head", core_pairs))
    feature = jax.ShapeDtypeStruct((rows // 4, 2 * columns + LANES), BF16)
    first, second, place = ordered(
        functools.partial(norm_kernel, slots, rank_rows),
        (),
        (ids, stream, input_norm_gain.reshape(-1, LANES), adapter_down_weight),
        [whole(ids.shape), pl.BlockSpec(memory_space=pltpu.HBM),
         whole((width_in // LANES, LANES)), pl.BlockSpec(memory_space=pltpu.HBM)],
        58,
        out_shape=[feature, feature, jax.ShapeDtypeStruct((rows, rows), BF16)],
        scratch_shapes=[
            pltpu.VMEM((rows, width_in), BF16),
            pltpu.VMEM((rows, width_in), BF16),
            pltpu.VMEM(adapter_down_weight.shape, BF16),
            pltpu.SemaphoreType.DMA((rows // CHUNK,)),
            pltpu.SemaphoreType.DMA,
        ],
    )
    near = [first, second]

    def swap(send, pairs, batch):
        return lax.ppermute(send.reshape(batch, -1, send.shape[-1]), "head", pairs)

    def split(keep, got, batch, after):
        return halve(keep.reshape(batch, -1, keep.shape[-1]), got, 3, after)

    rest = planes - 1

    def relay(piece, after):
        return ordered(
            pack_kernel,
            after,
            (piece,),
            [whole(piece.shape)],
            16,
            out_shape=jax.ShapeDtypeStruct(piece.shape, BF16),
        )

    beside, beyond = across(first, 1), across(first, 2)
    own_keep, own_send = project(near, weights, ups)
    far0 = [beside, beyond, across(relay(beyond, (own_send, beside)), 1)]
    later = relay(second, (far0[2],))
    beside, beyond = across(later, 1), across(later, 2)
    own_got = swap(own_send, first_pairs, 2)
    keep0, send0 = project(far0, weights, ups, (own_send, later))
    got0 = swap(send0, first_pairs, rest)
    own_keep, own_send = split(own_keep, own_got, 2, (send0,))
    own_got = swap(own_send, second_pairs, 2)
    depth = accepted.shape[1]
    masks, chosen = ordered(
        functools.partial(prep_kernel, slots, planes, rows),
        (own_send,),
        (ids, parents, accepted),
        [whole(ids.shape), whole(parents.shape), whole(accepted.shape)],
        16,
        out_shape=[
            jax.ShapeDtypeStruct((2, NODES, NODES), F32),
            jax.ShapeDtypeStruct((2, depth, NODES), F32),
        ],
    )
    far1 = [beside, beyond, across(relay(beyond, (send0, beside)), 1)]
    keep1, send1 = project(far1, weights, ups, (chosen,))
    got1 = swap(send1, first_pairs, rest)
    keep0, send0 = split(keep0, got0, rest, (send1,))
    got0 = swap(send0, second_pairs, rest)
    keep1, send1 = split(keep1, got1, rest, (send0,))
    got1 = swap(send1, second_pairs, rest)
    triple = join(0, (own_keep, own_got), (keep0, got0), 3, (send1,))
    out0, kept0 = attend(0, cache_length, triple, masks, chosen, key_value_cache)

    def spread_out(out):
        away_first = lax.ppermute(out, "head", first_pairs)
        away_second = lax.ppermute(out, "head", second_pairs)
        away_both = lax.ppermute(out, "head", [(h, h ^ 6) for h in range(owners)])
        return (out, away_second, away_first, away_both)

    side0 = spread_out(out0)
    triple = join(1, (own_keep, own_got), (keep1, got1), 3, (out0,))
    out1, kept1 = attend(1, cache_length, triple, masks, chosen, key_value_cache)
    side1 = spread_out(out1)

    def other_core(packed):
        return packed, lax.ppermute(packed, "head", core_pairs)

    own0, away0 = lift(other_core(pack(side0, (out1,))), planes, slots, down)
    home0 = across(away0, 1)
    own0, away0, packed = settle(own0, home0, (pack(side1, (own0,)),))
    home0 = across(away0, 2)
    own1, away1 = lift(other_core(packed), planes, slots, down)
    own1, away1 = settle(own1, across(away1, 1))
    home1 = across(away1, 2)
    operands = (place, own0, home0, own1, home1)
    attended = ordered(
        final_kernel,
        (),
        operands,
        [whole(operand.shape) for operand in operands],
        16,
        out_shape=jax.ShapeDtypeStruct((output_weight.shape[1], rows), BF16),
    )
    return jnp.swapaxes(attended, 0, 1), jnp.stack([kept0, kept1], axis=1)


def ancestors_of(parents):
    parent_links = jax.nn.one_hot(parents, NODES, dtype=jnp.float32)
    identity_matrix = jnp.eye(NODES, dtype=jnp.float32)
    ancestry = jnp.minimum(identity_matrix[None] + parent_links, 1.0)
    for squaring in range(NODES.bit_length()):
        ancestry = jnp.minimum(
            jnp.einsum("rnm,rmk->rnk", ancestry, ancestry, precision=lax.Precision.HIGHEST), 1.0
        )
    return ancestry


def plain_on_device(
    stream,
    row_tree_nodes,
    input_norm_gain,
    query_key_value_weight,
    adapter_down_weight,
    adapter_up_weight,
    key_value_cache,
    cache_length,
    parents,
    accepted,
    output_weight,
):
    owner_index = lax.axis_index("head")
    feature_rows = query_key_value_weight.shape[0]
    device_width = query_key_value_weight.shape[2]
    adapter_rank_rows = adapter_up_weight.shape[0]
    local_heads = device_width // HEAD_SIZE
    request_count = key_value_cache.shape[1]
    cache_span = key_value_cache.shape[2]
    wide_rows = stream.astype(jnp.float32)
    inverse_rms = lax.rsqrt(jnp.mean(wide_rows * wide_rows, axis=1, keepdims=True) + 1e-05)
    normalized_input = (wide_rows * inverse_rms * input_norm_gain.astype(jnp.float32)).astype(
        jnp.bfloat16
    )
    reduced_rank_rows = jnp.dot(
        normalized_input, adapter_down_weight, preferred_element_type=jnp.float32
    ).astype(jnp.bfloat16)
    feature_block = lax.dynamic_slice_in_dim(
        normalized_input, owner_index * feature_rows, feature_rows, 1
    )
    rank_block = lax.dynamic_slice_in_dim(
        reduced_rank_rows, owner_index * adapter_rank_rows, adapter_rank_rows, 1
    )
    gathered_features, gathered_ranks = (
        lax.all_gather(feature_block, "tok", axis=0, tiled=True),
        lax.all_gather(rank_block, "tok", axis=0, tiled=True),
    )
    projection = query_key_value_weight.reshape(feature_rows, 3 * device_width)
    lifting_matrix = adapter_up_weight.reshape(adapter_rank_rows, 3 * device_width)
    node_to_row = jnp.argsort(row_tree_nodes)
    part_sum = jnp.dot(
        gathered_features[node_to_row], projection, preferred_element_type=jnp.float32
    )
    node_rows = lax.psum_scatter(
        part_sum
        + jnp.dot(gathered_ranks[node_to_row], lifting_matrix, preferred_element_type=jnp.float32),
        "head",
        scatter_dimension=0,
        tiled=True,
    ).astype(jnp.bfloat16)
    triple = node_rows.reshape(request_count, NODES, 3, local_heads, HEAD_SIZE)
    queries = triple[:, :, 0]
    tree_key_rows = triple[:, :, 1]
    tree_value_rows = triple[:, :, 2]
    ancestry = ancestors_of(parents)
    attention_score_scale = HEAD_SIZE ** (-0.5)
    tree_score_matrix = (
        jnp.einsum("rnhd,rmhd->rhnm", queries, tree_key_rows, preferred_element_type=jnp.float32)
        * attention_score_scale
    )
    tree_score_matrix = jnp.where(ancestry[:, None] > 0.5, tree_score_matrix, -jnp.inf)
    keys_cache = key_value_cache[0].reshape(request_count, cache_span, local_heads, HEAD_SIZE)
    values_cache = key_value_cache[1].reshape(request_count, cache_span, local_heads, HEAD_SIZE)
    scores = (
        jnp.einsum("rnhd,rchd->rhnc", queries, keys_cache, preferred_element_type=jnp.float32)
        * attention_score_scale
    )
    positions = lax.broadcasted_iota(jnp.int32, (1, 1, 1, cache_span), 3)
    scores = jnp.where(positions < cache_length[:, None, None, None], scores, -jnp.inf)
    tree_top = jnp.max(tree_score_matrix, axis=-1, keepdims=True)
    largest = jnp.maximum(tree_top, jnp.max(scores, axis=-1, keepdims=True))
    cache_exp = jnp.exp(scores - largest)
    tree_exp = jnp.exp(tree_score_matrix - largest)
    totals = jnp.sum(cache_exp, axis=-1, keepdims=True) + jnp.sum(tree_exp, axis=-1, keepdims=True)
    cache_weights = (cache_exp / totals).astype(jnp.bfloat16)
    tree_weight_matrix = (tree_exp / totals).astype(jnp.bfloat16)
    attention = jnp.einsum(
        "rhnc,rchd->rnhd", cache_weights, values_cache, preferred_element_type=jnp.float32
    )
    attention = attention + jnp.einsum(
        "rhnm,rmhd->rnhd", tree_weight_matrix, tree_value_rows, preferred_element_type=jnp.float32
    )
    head_rows = attention.astype(jnp.bfloat16).reshape(request_count * NODES, device_width)
    node_table = node_rows.reshape(request_count, NODES, 3, device_width)
    chosen = jnp.take_along_axis(node_table, accepted[:, :, None, None], axis=1)
    accepted_kv = jnp.stack([chosen[:, :, 1], chosen[:, :, 2]])
    everything = lax.all_gather(head_rows, "head", axis=0, tiled=True)
    attended = lax.psum_scatter(
        jnp.dot(
            everything[row_tree_nodes], output_weight, preferred_element_type=jnp.float32
        ).astype(jnp.bfloat16),
        "tok",
        scatter_dimension=0,
        tiled=True,
    )
    return (attended, accepted_kv)


def solution(mesh):
    placed = (
        P("tok", None),
        P(),
        P(),
        P("head", None, "tok"),
        P(),
        P("head", None, "tok"),
        P(None, "head", None, "tok"),
        P("head"),
        P("head", None),
        P("head", None),
        P("tok", "head"),
    )
    sized = mesh.shape["head"] == 8 and mesh.shape["tok"] == 4
    return jax.shard_map(
        on_device if sized else plain_on_device,
        mesh=mesh,
        in_specs=placed,
        out_specs=(P("tok", "head"), P(None, "head", None, "tok")),
        check_vma=False,
    )
```

```python
import functools

import jax
import jax.numpy as jnp
from jax import lax
from jax.experimental import pallas as pl
from jax.experimental.pallas import tpu as pltpu
from jax.sharding import PartitionSpec as P

HEAD_SIZE = 224
NODES = 64
LANES = 128
F32 = jnp.float32
BF16 = jnp.bfloat16
SMALL = pl.CostEstimate(flops=1, bytes_accessed=1, transcendentals=0)
LARGE = pl.CostEstimate(flops=2 * 10**11, bytes_accessed=1, transcendentals=0)


def dot(a, b, dims=((1,), (0,))):
    return lax.dot_general(a, b, (dims, ((), ())), preferred_element_type=F32)


def whole(shape):
    return pl.BlockSpec(shape, lambda *_: (0,) * len(shape))


def ordered(kernel, after, operands, in_specs, megabytes, cost=SMALL, **options):
    count = len(after)

    def body(*refs):
        kernel(*refs[count:])

    return pl.pallas_call(
        body,
        in_specs=[pl.BlockSpec(memory_space=pl.ANY)] * count + in_specs,
        compiler_params=pltpu.CompilerParams(vmem_limit_bytes=megabytes * 2**20),
        cost_estimate=cost,
        **options,
    )(*after, *operands)


def row_to_column(row):
    size = row.shape[1]
    eye = lax.broadcasted_iota(jnp.int32, (size, size), 0) == lax.broadcasted_iota(
        jnp.int32, (size, size), 1
    )
    return jnp.sum(jnp.where(eye, row, 0), axis=1, keepdims=True)


def rank_in_plane(row):
    before = row_to_column(row) < row
    return jnp.sum(before.astype(jnp.int32), axis=0, keepdims=True)


def plane_row(ids_ref, plane, rows):
    per = rows // LANES
    parts = [ids_ref[pl.ds(plane * per + i, 1), :] for i in range(per)]
    return jnp.concatenate(parts, axis=1)


CHUNK = 32


def norm_kernel(slots, rank_rows, ids_ref, stream_hbm, gain_ref, down_hbm, feature_ref,
                place_ref, normed, held, down_ref, arrived, down_arrived):
    me = lax.axis_index("head")
    plane = lax.axis_index("tok")
    rows, width = held.shape
    copies = [
        pltpu.make_async_copy(
            stream_hbm.at[pl.ds(i * CHUNK, CHUNK), :],
            held.at[pl.ds(i * CHUNK, CHUNK), :],
            arrived.at[i],
        )
        for i in range(rows // CHUNK)
    ]
    for copy in copies:
        copy.start()
    down_copy = pltpu.make_async_copy(down_hbm, down_ref, down_arrived)
    down_copy.start()
    gains = gain_ref[...].astype(F32)
    gain = jnp.concatenate([gains[i : i + 1] for i in range(width // LANES)], axis=1)

    def norm(i, carry):
        at = pl.ds(pl.multiple_of(i * CHUNK, CHUNK), CHUNK)
        pltpu.make_async_copy(stream_hbm.at[at, :], held.at[at, :], arrived.at[i]).wait()
        wide = held[at, :].astype(F32)
        rstd = lax.rsqrt(jnp.sum(wide * wide, axis=1, keepdims=True) / width + 1e-05)
        normed[at, :] = (wide * rstd * gain).astype(BF16)
        return carry

    lax.fori_loop(0, rows // CHUNK, norm, 0)
    down_copy.wait()
    low = dot(normed[...], down_ref[...]).astype(BF16)
    ranks = low.shape[1]
    lane = lax.broadcasted_iota(jnp.int32, (ranks, LANES), 1)
    wanted = jnp.where(lane < rank_rows, me * rank_rows + lane, (me ^ 1) * rank_rows + lane - rank_rows)
    pick = lax.broadcasted_iota(jnp.int32, (ranks, LANES), 0) == wanted
    pick &= lane < 2 * rank_rows
    low = dot(low, pick.astype(BF16)).astype(BF16)
    ids = plane_row(ids_ref, plane, rows)
    rank = rank_in_plane(ids)
    owner = ids // (2 * NODES)
    second = (ids // NODES) % 2
    apart = owner ^ me
    even = (owner & 1) == 0
    bit_x = (apart >> 1) & 1
    bit_y = (apart >> 2) & 1
    order = (apart & 1) * 4 + jnp.where(even, bit_x * 2 + bit_y, bit_y * 2 + bit_x)
    half = rows // 2
    position = second * half + order * slots + rank % slots
    place_ref[...] = (
        lax.broadcasted_iota(jnp.int32, (rows, rows), 0) == position
    ).astype(BF16)
    quarter = half // 2
    position = jnp.where(order < 4, second * quarter + order * slots + rank % slots, -1)
    place = (lax.broadcasted_iota(jnp.int32, (half, rows), 0) == position).astype(BF16)
    columns = (feature_ref.shape[1] - LANES) // 2
    for i, owner_of in enumerate((me, me ^ 1)):
        block = normed[:, pl.ds(pl.multiple_of(owner_of * columns, LANES), columns)]
        feature_ref[:, i * columns : (i + 1) * columns] = dot(place, block).astype(BF16)
    feature_ref[:, 2 * columns :] = dot(place, low).astype(BF16)


def prep_kernel(slots, planes, rows, ids_ref, parents_ref, accepted_ref, mask_ref, chosen_ref):
    me = lax.axis_index("head")
    plane = lax.axis_index("tok")
    for j in range(2):
        nodes = []
        for k in range(planes):
            ids = plane_row(ids_ref, plane ^ k, rows)
            rank = rank_in_plane(ids)
            spot = lax.broadcasted_iota(jnp.int32, (slots, rows), 0) + (me * 2 + j) * slots
            nodes.append(
                jnp.sum(jnp.where(rank == spot, ids, 0), axis=1, keepdims=True)
                - (me * 2 + j) * NODES
            )
        nodes = jnp.concatenate(nodes, axis=0)
        lanes = lax.broadcasted_iota(jnp.int32, (NODES, NODES), 1)
        rows_of = lax.broadcasted_iota(jnp.int32, (NODES, NODES), 0)
        named = (nodes == lanes).astype(BF16)
        parent = row_to_column(parents_ref[j : j + 1, :])
        reach = ((parent == lanes) | (rows_of == lanes)).astype(BF16)
        for _ in range((NODES - 1).bit_length()):
            reach = jnp.minimum(dot(reach, reach), 1.0).astype(BF16)
        mask_ref[j] = dot(dot(named, reach).astype(BF16), named, ((1,), (1,)))
        accepted = row_to_column(accepted_ref[j : j + 1, :])
        depth = accepted.shape[0]
        wanted = (accepted == lax.broadcasted_iota(jnp.int32, (depth, NODES), 1)).astype(BF16)
        chosen_ref[j] = dot(wanted, named, ((1,), (1,)))


def tiles_of(width):
    first = (width // 512 + 1) * 256 if width % 512 else width // 2
    return [(0, first), (first, width - first)]


def project_kernel(pieces, *refs):
    lhs_refs = refs[:pieces]
    weight_refs = refs[pieces : pieces + 2]
    up_refs = refs[pieces + 2 : pieces + 4]
    keep_hbm, send_hbm = refs[pieces + 4 : pieces + 6]
    lhs, held, keep, send, arrived, left = refs[-6:]
    parts, columns, width = weight_refs[0].shape
    deep = held.shape[1]
    half = lhs.shape[0] // 2
    rank_rows = up_refs[0].shape[1]
    steps = [(p, start, size) for p in range(parts) for start, size in tiles_of(width)]

    def inward(i, side):
        p, start, size = steps[i]
        return pltpu.make_async_copy(
            weight_refs[side].at[p, :, pl.ds(start, size)],
            held.at[p, pl.ds(side * columns, columns), pl.ds(start, size)],
            arrived.at[i, side],
        )

    for i in range(len(steps)):
        for side in range(2):
            inward(i, side).start()
    at = 0
    for lhs_ref in lhs_refs:
        rows = lhs_ref.shape[0] // 4
        for j in range(2):
            lhs[at : at + rows, :] = lhs_ref[2 * j * rows : (2 * j + 1) * rows, :]
            lhs[half + at : half + at + rows, :] = lhs_ref[
                (2 * j + 1) * rows : (2 * j + 2) * rows, :
            ]
            at += rows
    for p in range(parts):
        low = 2 * columns
        for side in range(2):
            held[p, low : low + rank_rows, :] = up_refs[side][p]
            low += rank_rows
        held[p, low:, :] = jnp.zeros((deep - low, width), BF16)
    outward = []
    for i, (p, start, size) in enumerate(steps):
        for side in range(2):
            inward(i, side).wait()
        lanes = slice(p * width + start, p * width + start + size)
        total = dot(lhs[...], held[p, :, start : start + size])
        keep[:, lanes] = total[:half]
        send[:, lanes] = total[half:].astype(BF16)
        for j, (source, target) in enumerate(((keep, keep_hbm), (send, send_hbm))):
            copy = pltpu.make_async_copy(source.at[:, lanes], target.at[:, lanes], left.at[i, j])
            copy.start()
            outward.append(copy)
    for copy in outward:
        copy.wait()


def project(pieces, weights, ups, after=()):
    parts, columns, width = weights[0].shape
    steps = parts * len(tiles_of(width))
    rows = sum(piece.shape[0] for piece in pieces) // 2
    deep = pieces[0].shape[1]
    far = pl.BlockSpec(memory_space=pltpu.HBM)
    return ordered(
        functools.partial(project_kernel, len(pieces)),
        after,
        (*pieces, *weights, *ups),
        [whole(piece.shape) for piece in pieces] + [far] * 2 + [whole(ups[0].shape)] * 2,
        55,
        LARGE,
        out_specs=[far] * 2,
        out_shape=[
            jax.ShapeDtypeStruct((rows, parts * width), F32),
            jax.ShapeDtypeStruct((rows, parts * width), BF16),
        ],
        scratch_shapes=[
            pltpu.VMEM((2 * rows, deep), BF16),
            pltpu.VMEM((parts, deep, width), BF16),
            pltpu.VMEM((rows, parts * width), F32),
            pltpu.VMEM((rows, parts * width), BF16),
            pltpu.SemaphoreType.DMA((steps, 2)),
            pltpu.SemaphoreType.DMA((steps, 2)),
        ],
    )


def halve_kernel(keep_ref, got_ref, kept_ref, send_ref):
    added = keep_ref[...] + got_ref[...].astype(F32)
    half = added.shape[1] // 2
    kept_ref[...] = added[:, :half]
    send_ref[...] = added[:, half:].astype(BF16)


def halve(keep, got, parts, after=()):
    batch, rows, wide = keep.shape
    tile = wide // parts
    half = rows // 2

    def block(rows):
        return pl.BlockSpec((batch, rows, tile), lambda c: (0, 0, c))

    return ordered(
        halve_kernel,
        after,
        (keep, got),
        [block(rows)] * 2,
        16,
        grid=(parts,),
        out_specs=[block(half)] * 2,
        out_shape=[
            jax.ShapeDtypeStruct((batch, half, wide), F32),
            jax.ShapeDtypeStruct((batch, half, wide), BF16),
        ],
    )


def pass_kernel(*refs):
    pass


def pass_on(array, after):
    return ordered(
        pass_kernel,
        (*after, array),
        (),
        [],
        16,
        out_specs=pl.BlockSpec(memory_space=pl.ANY),
        out_shape=jax.ShapeDtypeStruct(array.shape, array.dtype),
        input_output_aliases={len(after): 0},
    )


def join_kernel(*refs):
    out_ref = refs[-1]
    slots = refs[0].shape[-2]
    at = 0
    for keep_ref, got_ref in zip(refs[:-1:2], refs[1:-1:2]):
        for k in range(keep_ref.shape[0]):
            out_ref[at : at + slots] = (keep_ref[k] + got_ref[k].astype(F32)).astype(BF16)
            at += slots


def join(j, pairs, parts, after=()):
    slots, wide = pairs[0][0].shape[1:]
    tile = wide // parts
    specs = []
    operands = []
    for pair in pairs:
        planes = pair[0].shape[0] // 2
        spec = pl.BlockSpec((planes, None, slots, tile), lambda c: (0, j, 0, c))
        specs += [spec, spec]
        operands += [array.reshape(planes, 2, slots, wide) for array in pair]
    rows = sum(pair[0].shape[0] for pair in pairs) // 2 * slots
    return ordered(
        join_kernel,
        after,
        operands,
        specs,
        16,
        grid=(parts,),
        out_specs=pl.BlockSpec((rows, tile), lambda c: (0, c)),
        out_shape=jax.ShapeDtypeStruct((rows, wide), BF16),
    )


HEADS = 4
LOG2E = 1.4426950408889634


def attend_kernel(j, span, groups, length_ref, triple_ref, mask_ref, chosen_ref, cache_ref,
                  out_ref, kept_ref, spread, top, total, acc, held, arrived):
    chunks = held.shape[1]
    tile = spread.shape[2]
    width = groups * tile
    length = length_ref[j]
    scale = HEAD_SIZE ** (-0.5) * LOG2E

    def copy(part, c):
        return pltpu.make_async_copy(
            cache_ref.at[part, j, pl.ds(c * span, span), :], held.at[part, c], arrived.at[part, c]
        )

    for c in range(chunks):
        @pl.when(c * span < length)
        def fetch():
            copy(0, c).start()
            copy(1, c).start()

    head_of_lane = lax.broadcasted_iota(jnp.int32, (1, tile), 1) // HEAD_SIZE

    def fold(g, scores, values, first):
        peak = jnp.max(scores, axis=1, keepdims=True)
        if not first:
            before = top[g]
            peak = jnp.maximum(before, peak)
        weights = jnp.exp2(scores - peak)
        gained = jnp.sum(weights, axis=1, keepdims=True)
        part = dot(weights.astype(BF16), values)
        if first:
            total[g] = gained
            acc[g] = part
        else:
            shrink = jnp.exp2(before - peak)
            total[g] = total[g] * shrink + gained
            acc[g] = acc[g] * shrink + part
        top[g] = peak

    allowed = jnp.concatenate([mask_ref[j]] * HEADS, axis=0) > 0.5
    pick = chosen_ref[j].astype(BF16)
    for g in range(groups):
        lanes = slice(g * tile, (g + 1) * tile)
        query = triple_ref[:, lanes]
        keys = triple_ref[:, width + g * tile : width + (g + 1) * tile]
        values = triple_ref[:, 2 * width + g * tile : 2 * width + (g + 1) * tile]
        for h in range(HEADS):
            spread[g, h * NODES : (h + 1) * NODES, :] = jnp.where(head_of_lane == h, query, 0)
        scores = dot(spread[g], keys, ((1,), (1,))) * scale
        fold(g, jnp.where(allowed, scores, -1e30), values, True)
        kept_ref[0, :, lanes] = dot(pick, keys).astype(BF16)
        kept_ref[1, :, lanes] = dot(pick, values).astype(BF16)

    for c in range(chunks):
        @pl.when(c * span < length)
        def cached():
            copy(0, c).wait()
            copy(1, c).wait()
            spot = lax.broadcasted_iota(jnp.int32, (1, span), 1) + c * span
            bias = jnp.where(spot < length, 0.0, -1e30)
            for g in range(groups):
                lanes = slice(g * tile, (g + 1) * tile)
                scores = dot(spread[g], held[0, c, :, lanes], ((1,), (1,)))
                fold(g, scores * scale + bias, held[1, c, :, lanes], False)

    for g in range(groups):
        share = acc[g] / total[g]
        out = jnp.zeros((NODES, tile), F32)
        for h in range(HEADS):
            out = jnp.where(head_of_lane == h, share[h * NODES : (h + 1) * NODES, :], out)
        out_ref[:, g * tile : (g + 1) * tile] = out.astype(BF16)


def attend(j, lengths, triple, masks, chosen, cache, after=()):
    cache_span, width = cache.shape[2:]
    tile = HEADS * HEAD_SIZE
    groups = width // tile
    span = min(512, cache_span)
    chunks = cache_span // span
    depth = chosen.shape[1]
    return ordered(
        functools.partial(attend_kernel, j, span, groups),
        after,
        (lengths, triple, masks, chosen, cache),
        [
            pl.BlockSpec(memory_space=pltpu.SMEM),
            whole(triple.shape),
            whole(masks.shape),
            whole(chosen.shape),
            pl.BlockSpec(memory_space=pltpu.HBM),
        ],
        32,
        out_specs=[whole((NODES, width)), whole((2, depth, width))],
        out_shape=[
            jax.ShapeDtypeStruct((NODES, width), BF16),
            jax.ShapeDtypeStruct((2, depth, width), BF16),
        ],
        scratch_shapes=[
            pltpu.VMEM((groups, HEADS * NODES, tile), BF16),
            pltpu.VMEM((groups, HEADS * NODES, 1), F32),
            pltpu.VMEM((groups, HEADS * NODES, 1), F32),
            pltpu.VMEM((groups, HEADS * NODES, tile), F32),
            pltpu.VMEM((2, chunks, span, width), BF16),
            pltpu.SemaphoreType.DMA((2, chunks)),
        ],
    )


def pack_kernel(*refs):
    rows = refs[0].shape[0]
    for i, ref in enumerate(refs[:-1]):
        refs[-1][i * rows : (i + 1) * rows, :] = ref[...]


def pack(pieces, after=()):
    rows, width = pieces[0].shape
    return ordered(
        pack_kernel,
        after,
        pieces,
        [whole((rows, width))] * len(pieces),
        16,
        out_shape=jax.ShapeDtypeStruct((rows * len(pieces), width), BF16),
    )


def lift_kernel(planes, slots, *refs):
    pieces = refs[:-4]
    weight_ref, own_ref, other_ref, rows = refs[-4:]
    share = rows.shape[0] // planes
    for k in range(planes):
        at = k * share
        for piece in pieces:
            for q in range(piece.shape[0] // (planes * slots)):
                rows[at : at + slots, :] = piece[
                    (q * planes + k) * slots : (q * planes + k + 1) * slots, :
                ]
                at += slots
    lifted = dot(weight_ref[...], rows[...], ((1,), (1,)))
    for k in range(planes):
        piece = lifted[:, k * share : (k + 1) * share]
        if k % 2 == 0:
            own_ref[k // 2] = piece
        else:
            other_ref[k // 2] = piece.astype(BF16)


def lift(pieces, planes, slots, weight, after=()):
    wide, width = weight.shape
    rows = sum(piece.shape[0] for piece in pieces)
    return ordered(
        functools.partial(lift_kernel, planes, slots),
        after,
        (*pieces, weight),
        [whole(piece.shape) for piece in pieces] + [whole(weight.shape)],
        20,
        out_shape=[
            jax.ShapeDtypeStruct((planes // 2, wide, rows // planes), F32),
            jax.ShapeDtypeStruct((planes // 2, wide, rows // planes), BF16),
        ],
        scratch_shapes=[pltpu.VMEM((rows, width), BF16)],
    )


def settle_kernel(own_ref, got_ref, kept_ref, send_ref, *_):
    kept_ref[...] = own_ref[0] + got_ref[0].astype(F32)
    send_ref[...] = (own_ref[1] + got_ref[1].astype(F32)).astype(BF16)


def settle(own, got, passed=()):
    shape = own.shape[1:]
    return ordered(
        settle_kernel,
        passed,
        (own, got),
        [whole(own.shape)] * 2,
        16,
        out_specs=[whole(shape)] * 2 + [pl.BlockSpec(memory_space=pl.ANY)] * len(passed),
        out_shape=[jax.ShapeDtypeStruct(shape, F32), jax.ShapeDtypeStruct(shape, BF16)]
        + [jax.ShapeDtypeStruct(array.shape, array.dtype) for array in passed],
        input_output_aliases={i: 2 + i for i in range(len(passed))},
    )


def final_kernel(place_ref, *refs):
    sums = [
        (refs[2 * j][...] + refs[2 * j + 1][...].astype(F32)).astype(BF16) for j in range(2)
    ]
    refs[-1][...] = dot(jnp.concatenate(sums, axis=1), place_ref[...]).astype(BF16)


def on_device(
    stream,
    row_tree_nodes,
    input_norm_gain,
    query_key_value_weight,
    adapter_down_weight,
    adapter_up_weight,
    key_value_cache,
    cache_length,
    parents,
    accepted,
    output_weight,
):
    rows, width_in = stream.shape
    planes = row_tree_nodes.shape[0] // rows
    owners = width_in // query_key_value_weight.shape[0]
    slots = rows // (2 * owners)
    columns = query_key_value_weight.shape[0]
    width = query_key_value_weight.shape[2]
    rank_rows = adapter_up_weight.shape[0]
    weight = jnp.swapaxes(query_key_value_weight, 0, 1)
    up = jnp.swapaxes(adapter_up_weight, 0, 1)
    down = jnp.swapaxes(output_weight, 0, 1)
    ids = row_tree_nodes.reshape(-1, LANES)

    def first_mask(h):
        return 2 if h % 2 == 0 else 4

    core_pairs = [(h, h ^ 1) for h in range(owners)]
    first_pairs = [(h, h ^ first_mask(h)) for h in range(owners)]
    second_pairs = [(h, h ^ (6 - first_mask(h))) for h in range(owners)]

    def across(array, k):
        return lax.ppermute(array, "tok", [(z, z ^ k) for z in range(planes)])

    weights = (weight, lax.ppermute(weight, "head", core_pairs))
    ups = (up, lax.ppermute(up, "head", core_pairs))
    feature, place = ordered(
        functools.partial(norm_kernel, slots, rank_rows),
        (),
        (ids, stream, input_norm_gain.reshape(-1, LANES), adapter_down_weight),
        [whole(ids.shape), pl.BlockSpec(memory_space=pltpu.HBM),
         whole((width_in // LANES, LANES)), pl.BlockSpec(memory_space=pltpu.HBM)],
        62,
        out_shape=[
            jax.ShapeDtypeStruct((rows // 2, 2 * columns + LANES), BF16),
            jax.ShapeDtypeStruct((rows, rows), BF16),
        ],
        scratch_shapes=[
            pltpu.VMEM((rows, width_in), BF16),
            pltpu.VMEM((rows, width_in), BF16),
            pltpu.VMEM(adapter_down_weight.shape, BF16),
            pltpu.SemaphoreType.DMA((rows // CHUNK,)),
            pltpu.SemaphoreType.DMA,
        ],
    )

    def swap(send, pairs, batch):
        return lax.ppermute(send.reshape(batch, -1, send.shape[-1]), "head", pairs)

    def split(keep, got, batch, after=()):
        return halve(keep.reshape(batch, -1, keep.shape[-1]), got, 3, after)

    beyond, beside = across(feature, 2), across(feature, 1)
    own_keep, own_send = project([feature], weights, ups)
    own_got = swap(own_send, first_pairs, 2)
    depth = accepted.shape[1]
    masks, chosen = ordered(
        functools.partial(prep_kernel, slots, planes, rows),
        (own_send,),
        (ids, parents, accepted),
        [whole(ids.shape), whole(parents.shape), whole(accepted.shape)],
        16,
        out_shape=[
            jax.ShapeDtypeStruct((2, NODES, NODES), F32),
            jax.ShapeDtypeStruct((2, depth, NODES), F32),
        ],
    )
    onward = pass_on(beyond, (chosen, beside))
    furthest = across(onward, 1)
    mid_keep, mid_send = project([beside, onward], weights, ups)
    mid_got = swap(mid_send, first_pairs, 4)
    own_keep, own_send = split(own_keep, own_got, 2, (mid_send,))
    own_got = swap(own_send, second_pairs, 2)
    far_keep, far_send = project([furthest], weights, ups, (own_send,))
    far_got = swap(far_send, first_pairs, 2)
    mid_keep, mid_send = split(mid_keep, mid_got, 4, (far_send,))
    mid_got = swap(mid_send, second_pairs, 4)
    far_keep, far_send = split(far_keep, far_got, 2, (mid_send,))
    far_got = swap(far_send, second_pairs, 2)
    pairs = ((own_keep, own_got), (mid_keep, mid_got), (far_keep, far_got))
    triple = join(0, pairs, 3)
    out0, kept0 = attend(0, cache_length, triple, masks, chosen, key_value_cache)

    def spread_out(out):
        away_first = lax.ppermute(out, "head", first_pairs)
        away_second = lax.ppermute(out, "head", second_pairs)
        away_both = lax.ppermute(out, "head", [(h, h ^ 6) for h in range(owners)])
        return (out, away_second, away_first, away_both)

    side0 = spread_out(out0)
    triple = join(1, pairs, 3, (out0,))
    out1, kept1 = attend(1, cache_length, triple, masks, chosen, key_value_cache)
    side1 = spread_out(out1)

    def other_core(packed):
        return packed, lax.ppermute(packed, "head", core_pairs)

    own0, away0 = lift(other_core(pack(side0, (out1,))), planes, slots, down)
    home0 = across(away0, 1)
    own0, away0, packed = settle(own0, home0, (pack(side1, (own0,)),))
    home0 = across(away0, 2)
    own1, away1 = lift(other_core(packed), planes, slots, down)
    own1, away1 = settle(own1, across(away1, 1))
    home1 = across(away1, 2)
    operands = (place, own0, home0, own1, home1)
    attended = ordered(
        final_kernel,
        (),
        operands,
        [whole(operand.shape) for operand in operands],
        16,
        out_shape=jax.ShapeDtypeStruct((output_weight.shape[1], rows), BF16),
    )
    return jnp.swapaxes(attended, 0, 1), jnp.stack([kept0, kept1], axis=1)


def ancestors_of(parents):
    parent_links = jax.nn.one_hot(parents, NODES, dtype=jnp.float32)
    identity_matrix = jnp.eye(NODES, dtype=jnp.float32)
    ancestry = jnp.minimum(identity_matrix[None] + parent_links, 1.0)
    for squaring in range(NODES.bit_length()):
        ancestry = jnp.minimum(
            jnp.einsum("rnm,rmk->rnk", ancestry, ancestry, precision=lax.Precision.HIGHEST), 1.0
        )
    return ancestry


def plain_on_device(
    stream,
    row_tree_nodes,
    input_norm_gain,
    query_key_value_weight,
    adapter_down_weight,
    adapter_up_weight,
    key_value_cache,
    cache_length,
    parents,
    accepted,
    output_weight,
):
    owner_index = lax.axis_index("head")
    feature_rows = query_key_value_weight.shape[0]
    device_width = query_key_value_weight.shape[2]
    adapter_rank_rows = adapter_up_weight.shape[0]
    local_heads = device_width // HEAD_SIZE
    request_count = key_value_cache.shape[1]
    cache_span = key_value_cache.shape[2]
    wide_rows = stream.astype(jnp.float32)
    inverse_rms = lax.rsqrt(jnp.mean(wide_rows * wide_rows, axis=1, keepdims=True) + 1e-05)
    normalized_input = (wide_rows * inverse_rms * input_norm_gain.astype(jnp.float32)).astype(
        jnp.bfloat16
    )
    reduced_rank_rows = jnp.dot(
        normalized_input, adapter_down_weight, preferred_element_type=jnp.float32
    ).astype(jnp.bfloat16)
    feature_block = lax.dynamic_slice_in_dim(
        normalized_input, owner_index * feature_rows, feature_rows, 1
    )
    rank_block = lax.dynamic_slice_in_dim(
        reduced_rank_rows, owner_index * adapter_rank_rows, adapter_rank_rows, 1
    )
    gathered_features, gathered_ranks = (
        lax.all_gather(feature_block, "tok", axis=0, tiled=True),
        lax.all_gather(rank_block, "tok", axis=0, tiled=True),
    )
    projection = query_key_value_weight.reshape(feature_rows, 3 * device_width)
    lifting_matrix = adapter_up_weight.reshape(adapter_rank_rows, 3 * device_width)
    node_to_row = jnp.argsort(row_tree_nodes)
    part_sum = jnp.dot(
        gathered_features[node_to_row], projection, preferred_element_type=jnp.float32
    )
    node_rows = lax.psum_scatter(
        part_sum
        + jnp.dot(gathered_ranks[node_to_row], lifting_matrix, preferred_element_type=jnp.float32),
        "head",
        scatter_dimension=0,
        tiled=True,
    ).astype(jnp.bfloat16)
    triple = node_rows.reshape(request_count, NODES, 3, local_heads, HEAD_SIZE)
    queries = triple[:, :, 0]
    tree_key_rows = triple[:, :, 1]
    tree_value_rows = triple[:, :, 2]
    ancestry = ancestors_of(parents)
    attention_score_scale = HEAD_SIZE ** (-0.5)
    tree_score_matrix = (
        jnp.einsum("rnhd,rmhd->rhnm", queries, tree_key_rows, preferred_element_type=jnp.float32)
        * attention_score_scale
    )
    tree_score_matrix = jnp.where(ancestry[:, None] > 0.5, tree_score_matrix, -jnp.inf)
    keys_cache = key_value_cache[0].reshape(request_count, cache_span, local_heads, HEAD_SIZE)
    values_cache = key_value_cache[1].reshape(request_count, cache_span, local_heads, HEAD_SIZE)
    scores = (
        jnp.einsum("rnhd,rchd->rhnc", queries, keys_cache, preferred_element_type=jnp.float32)
        * attention_score_scale
    )
    positions = lax.broadcasted_iota(jnp.int32, (1, 1, 1, cache_span), 3)
    scores = jnp.where(positions < cache_length[:, None, None, None], scores, -jnp.inf)
    tree_top = jnp.max(tree_score_matrix, axis=-1, keepdims=True)
    largest = jnp.maximum(tree_top, jnp.max(scores, axis=-1, keepdims=True))
    cache_exp = jnp.exp(scores - largest)
    tree_exp = jnp.exp(tree_score_matrix - largest)
    totals = jnp.sum(cache_exp, axis=-1, keepdims=True) + jnp.sum(tree_exp, axis=-1, keepdims=True)
    cache_weights = (cache_exp / totals).astype(jnp.bfloat16)
    tree_weight_matrix = (tree_exp / totals).astype(jnp.bfloat16)
    attention = jnp.einsum(
        "rhnc,rchd->rnhd", cache_weights, values_cache, preferred_element_type=jnp.float32
    )
    attention = attention + jnp.einsum(
        "rhnm,rmhd->rnhd", tree_weight_matrix, tree_value_rows, preferred_element_type=jnp.float32
    )
    head_rows = attention.astype(jnp.bfloat16).reshape(request_count * NODES, device_width)
    node_table = node_rows.reshape(request_count, NODES, 3, device_width)
    chosen = jnp.take_along_axis(node_table, accepted[:, :, None, None], axis=1)
    accepted_kv = jnp.stack([chosen[:, :, 1], chosen[:, :, 2]])
    everything = lax.all_gather(head_rows, "head", axis=0, tiled=True)
    attended = lax.psum_scatter(
        jnp.dot(
            everything[row_tree_nodes], output_weight, preferred_element_type=jnp.float32
        ).astype(jnp.bfloat16),
        "tok",
        scatter_dimension=0,
        tiled=True,
    )
    return (attended, accepted_kv)


def solution(mesh):
    placed = (
        P("tok", None),
        P(),
        P(),
        P("head", None, "tok"),
        P(),
        P("head", None, "tok"),
        P(None, "head", None, "tok"),
        P("head"),
        P("head", None),
        P("head", None),
        P("tok", "head"),
    )
    sized = mesh.shape["head"] == 8 and mesh.shape["tok"] == 4
    return jax.shard_map(
        on_device if sized else plain_on_device,
        mesh=mesh,
        in_specs=placed,
        out_specs=(P("tok", "head"), P(None, "head", None, "tok")),
        check_vma=False,
    )
```

```python
import functools

import jax
import jax.numpy as jnp
from jax import lax
from jax.experimental import pallas as pl
from jax.experimental.pallas import tpu as pltpu
from jax.sharding import PartitionSpec as P

HEAD_SIZE = 224
NODES = 64
LANES = 128
F32 = jnp.float32
BF16 = jnp.bfloat16
SMALL = pl.CostEstimate(flops=1, bytes_accessed=1, transcendentals=0)
LARGE = pl.CostEstimate(flops=2 * 10**11, bytes_accessed=1, transcendentals=0)


def dot(a, b, dims=((1,), (0,))):
    return lax.dot_general(a, b, (dims, ((), ())), preferred_element_type=F32)


def whole(shape):
    return pl.BlockSpec(shape, lambda *_: (0,) * len(shape))


def ordered(kernel, after, operands, in_specs, megabytes, cost=SMALL, **options):
    count = len(after)

    def body(*refs):
        kernel(*refs[count:])

    return pl.pallas_call(
        body,
        in_specs=[pl.BlockSpec(memory_space=pl.ANY)] * count + in_specs,
        compiler_params=pltpu.CompilerParams(vmem_limit_bytes=megabytes * 2**20),
        cost_estimate=cost,
        **options,
    )(*after, *operands)


def row_to_column(row):
    size = row.shape[1]
    eye = lax.broadcasted_iota(jnp.int32, (size, size), 0) == lax.broadcasted_iota(
        jnp.int32, (size, size), 1
    )
    return jnp.sum(jnp.where(eye, row, 0), axis=1, keepdims=True)


def rank_in_plane(row):
    before = row_to_column(row) < row
    return jnp.sum(before.astype(jnp.int32), axis=0, keepdims=True)


def plane_row(ids_ref, plane, rows):
    per = rows // LANES
    parts = [ids_ref[pl.ds(plane * per + i, 1), :] for i in range(per)]
    return jnp.concatenate(parts, axis=1)


CHUNK = 32


def norm_kernel(slots, rank_rows, ids_ref, stream_hbm, gain_ref, down_hbm, feature_ref,
                place_ref, normed, held, down_ref, arrived, down_arrived):
    me = lax.axis_index("head")
    plane = lax.axis_index("tok")
    rows, width = held.shape
    copies = [
        pltpu.make_async_copy(
            stream_hbm.at[pl.ds(i * CHUNK, CHUNK), :],
            held.at[pl.ds(i * CHUNK, CHUNK), :],
            arrived.at[i],
        )
        for i in range(rows // CHUNK)
    ]
    for copy in copies:
        copy.start()
    down_copy = pltpu.make_async_copy(down_hbm, down_ref, down_arrived)
    down_copy.start()
    gains = gain_ref[...].astype(F32)
    gain = jnp.concatenate([gains[i : i + 1] for i in range(width // LANES)], axis=1)

    def norm(i, carry):
        at = pl.ds(pl.multiple_of(i * CHUNK, CHUNK), CHUNK)
        pltpu.make_async_copy(stream_hbm.at[at, :], held.at[at, :], arrived.at[i]).wait()
        wide = held[at, :].astype(F32)
        rstd = lax.rsqrt(jnp.sum(wide * wide, axis=1, keepdims=True) / width + 1e-05)
        normed[at, :] = (wide * rstd * gain).astype(BF16)
        return carry

    lax.fori_loop(0, rows // CHUNK, norm, 0)
    down_copy.wait()
    low = dot(normed[...], down_ref[...]).astype(BF16)
    ranks = low.shape[1]
    lane = lax.broadcasted_iota(jnp.int32, (ranks, LANES), 1)
    wanted = jnp.where(lane < rank_rows, me * rank_rows + lane, (me ^ 1) * rank_rows + lane - rank_rows)
    pick = lax.broadcasted_iota(jnp.int32, (ranks, LANES), 0) == wanted
    pick &= lane < 2 * rank_rows
    low = dot(low, pick.astype(BF16)).astype(BF16)
    ids = plane_row(ids_ref, plane, rows)
    rank = rank_in_plane(ids)
    owner = ids // (2 * NODES)
    second = (ids // NODES) % 2
    apart = owner ^ me
    even = (owner & 1) == 0
    bit_x = (apart >> 1) & 1
    bit_y = (apart >> 2) & 1
    order = (apart & 1) * 4 + jnp.where(even, bit_x * 2 + bit_y, bit_y * 2 + bit_x)
    half = rows // 2
    position = second * half + order * slots + rank % slots
    place_ref[...] = (
        lax.broadcasted_iota(jnp.int32, (rows, rows), 0) == position
    ).astype(BF16)
    quarter = half // 2
    position = jnp.where(order < 4, second * quarter + order * slots + rank % slots, -1)
    place = (lax.broadcasted_iota(jnp.int32, (half, rows), 0) == position).astype(BF16)
    columns = (feature_ref.shape[1] - LANES) // 2
    for i, owner_of in enumerate((me, me ^ 1)):
        block = normed[:, pl.ds(pl.multiple_of(owner_of * columns, LANES), columns)]
        feature_ref[:, i * columns : (i + 1) * columns] = dot(place, block).astype(BF16)
    feature_ref[:, 2 * columns :] = dot(place, low).astype(BF16)


def prep_kernel(slots, planes, rows, ids_ref, parents_ref, accepted_ref, mask_ref, chosen_ref):
    me = lax.axis_index("head")
    plane = lax.axis_index("tok")
    for j in range(2):
        nodes = []
        for k in range(planes):
            ids = plane_row(ids_ref, plane ^ k, rows)
            rank = rank_in_plane(ids)
            spot = lax.broadcasted_iota(jnp.int32, (slots, rows), 0) + (me * 2 + j) * slots
            nodes.append(
                jnp.sum(jnp.where(rank == spot, ids, 0), axis=1, keepdims=True)
                - (me * 2 + j) * NODES
            )
        nodes = jnp.concatenate(nodes, axis=0)
        lanes = lax.broadcasted_iota(jnp.int32, (NODES, NODES), 1)
        rows_of = lax.broadcasted_iota(jnp.int32, (NODES, NODES), 0)
        named = (nodes == lanes).astype(BF16)
        parent = row_to_column(parents_ref[j : j + 1, :])
        reach = ((parent == lanes) | (rows_of == lanes)).astype(BF16)
        for _ in range((NODES - 1).bit_length()):
            reach = jnp.minimum(dot(reach, reach), 1.0).astype(BF16)
        mask_ref[j] = dot(dot(named, reach).astype(BF16), named, ((1,), (1,)))
        accepted = row_to_column(accepted_ref[j : j + 1, :])
        depth = accepted.shape[0]
        wanted = (accepted == lax.broadcasted_iota(jnp.int32, (depth, NODES), 1)).astype(BF16)
        chosen_ref[j] = dot(wanted, named, ((1,), (1,)))


def tiles_of(width):
    first = (width // 512 + 1) * 256 if width % 512 else width // 2
    return [(0, first), (first, width - first)]


def project_kernel(pieces, *refs):
    lhs_refs = refs[:pieces]
    weight_refs = refs[pieces : pieces + 2]
    up_refs = refs[pieces + 2 : pieces + 4]
    keep_hbm, send_hbm = refs[pieces + 4 : pieces + 6]
    lhs, held, keep, send, arrived, left = refs[-6:]
    parts, columns, width = weight_refs[0].shape
    deep = held.shape[1]
    half = lhs.shape[0] // 2
    rank_rows = up_refs[0].shape[1]
    steps = [(p, start, size) for p in range(parts) for start, size in tiles_of(width)]

    def inward(i, side):
        p, start, size = steps[i]
        return pltpu.make_async_copy(
            weight_refs[side].at[p, :, pl.ds(start, size)],
            held.at[p, pl.ds(side * columns, columns), pl.ds(start, size)],
            arrived.at[i, side],
        )

    for i in range(len(steps)):
        for side in range(2):
            inward(i, side).start()
    at = 0
    for lhs_ref in lhs_refs:
        rows = lhs_ref.shape[0] // 4
        for j in range(2):
            lhs[at : at + rows, :] = lhs_ref[2 * j * rows : (2 * j + 1) * rows, :]
            lhs[half + at : half + at + rows, :] = lhs_ref[
                (2 * j + 1) * rows : (2 * j + 2) * rows, :
            ]
            at += rows
    for p in range(parts):
        low = 2 * columns
        for side in range(2):
            held[p, low : low + rank_rows, :] = up_refs[side][p]
            low += rank_rows
        held[p, low:, :] = jnp.zeros((deep - low, width), BF16)
    outward = []
    for i, (p, start, size) in enumerate(steps):
        for side in range(2):
            inward(i, side).wait()
        lanes = slice(p * width + start, p * width + start + size)
        total = dot(lhs[...], held[p, :, start : start + size])
        keep[:, lanes] = total[:half]
        send[:, lanes] = total[half:].astype(BF16)
        for j, (source, target) in enumerate(((keep, keep_hbm), (send, send_hbm))):
            copy = pltpu.make_async_copy(source.at[:, lanes], target.at[:, lanes], left.at[i, j])
            copy.start()
            outward.append(copy)
    for copy in outward:
        copy.wait()


def project(pieces, weights, ups, after=()):
    parts, columns, width = weights[0].shape
    steps = parts * len(tiles_of(width))
    rows = sum(piece.shape[0] for piece in pieces) // 2
    deep = pieces[0].shape[1]
    far = pl.BlockSpec(memory_space=pltpu.HBM)
    return ordered(
        functools.partial(project_kernel, len(pieces)),
        after,
        (*pieces, *weights, *ups),
        [whole(piece.shape) for piece in pieces] + [far] * 2 + [whole(ups[0].shape)] * 2,
        55,
        LARGE,
        out_specs=[far] * 2,
        out_shape=[
            jax.ShapeDtypeStruct((rows, parts * width), F32),
            jax.ShapeDtypeStruct((rows, parts * width), BF16),
        ],
        scratch_shapes=[
            pltpu.VMEM((2 * rows, deep), BF16),
            pltpu.VMEM((parts, deep, width), BF16),
            pltpu.VMEM((rows, parts * width), F32),
            pltpu.VMEM((rows, parts * width), BF16),
            pltpu.SemaphoreType.DMA((steps, 2)),
            pltpu.SemaphoreType.DMA((steps, 2)),
        ],
    )


def pass_kernel(*refs):
    pass


def pass_on(array, after):
    return ordered(
        pass_kernel,
        (*after, array),
        (),
        [],
        16,
        out_specs=pl.BlockSpec(memory_space=pl.ANY),
        out_shape=jax.ShapeDtypeStruct(array.shape, array.dtype),
        input_output_aliases={len(after): 0},
    )


def part_kernel(keep_ref, got_ref, kept_ref, *send_refs):
    added = keep_ref[...] + got_ref[...].astype(F32)
    half = added.shape[1] // 2
    kept_ref[...] = added[:, :half]
    for b in range(added.shape[0]):
        send_refs[b % 2][b // 2] = added[b, half:].astype(BF16)


def part(keep, got, parts, after=()):
    batch, rows, wide = keep.shape
    tile = wide // parts
    half = rows // 2

    def block(batch, rows):
        return pl.BlockSpec((batch, rows, tile), lambda c: (0, 0, c))

    return ordered(
        part_kernel,
        after,
        (keep, got),
        [block(batch, rows)] * 2,
        16,
        grid=(parts,),
        out_specs=[block(batch, half)] + [block(batch // 2, half)] * 2,
        out_shape=[jax.ShapeDtypeStruct((batch, half, wide), F32)]
        + [jax.ShapeDtypeStruct((batch // 2, half, wide), BF16)] * 2,
    )


def join_kernel(*refs):
    out_ref = refs[-1]
    slots = refs[0].shape[-2]
    at = 0
    for keep_ref, got_ref in zip(refs[:-1:2], refs[1:-1:2]):
        for k in range(keep_ref.shape[0]):
            out_ref[at : at + slots] = (keep_ref[k] + got_ref[k].astype(F32)).astype(BF16)
            at += slots


def join(j, pairs, parts, after=()):
    slots, wide = pairs[0][0].shape[1:]
    tile = wide // parts
    specs = []
    operands = []
    for keep, got in pairs:
        planes = got.shape[0]
        specs.append(pl.BlockSpec((planes, None, slots, tile), lambda c: (0, j, 0, c)))
        specs.append(pl.BlockSpec((planes, slots, tile), lambda c: (0, 0, c)))
        operands += [keep.reshape(planes, 2, slots, wide), got]
    rows = sum(pair[1].shape[0] for pair in pairs) * slots
    return ordered(
        join_kernel,
        after,
        operands,
        specs,
        16,
        grid=(parts,),
        out_specs=pl.BlockSpec((rows, tile), lambda c: (0, c)),
        out_shape=jax.ShapeDtypeStruct((rows, wide), BF16),
    )


HEADS = 4
LOG2E = 1.4426950408889634


def attend_kernel(j, span, groups, length_ref, triple_ref, mask_ref, chosen_ref, cache_ref,
                  out_ref, kept_ref, spread, held, arrived):
    chunks = held.shape[1] // span
    tile = spread.shape[2]
    width = groups * tile
    length = length_ref[j]
    scale = HEAD_SIZE ** (-0.5) * LOG2E

    def copy(part, c):
        at = pl.ds(c * span, span)
        return pltpu.make_async_copy(
            cache_ref.at[part, j, at, :], held.at[part, at, :], arrived.at[part, c]
        )

    for part in range(2):
        for c in range(chunks):
            @pl.when(c * span < length)
            def fetch():
                copy(part, c).start()

    head_of_lane = lax.broadcasted_iota(jnp.int32, (1, tile), 1) // HEAD_SIZE
    pick = chosen_ref[j].astype(BF16)
    for g in range(groups):
        lanes = slice(g * tile, (g + 1) * tile)
        query = triple_ref[:, lanes]
        for h in range(HEADS):
            spread[g, h * NODES : (h + 1) * NODES, :] = jnp.where(head_of_lane == h, query, 0)
        for part in range(2):
            start = (part + 1) * width + g * tile
            kept_ref[part, :, lanes] = dot(pick, triple_ref[:, start : start + tile]).astype(BF16)

    def attend_to(count):
        allowed = jnp.concatenate([mask_ref[j]] * HEADS, axis=0) > 0.5
        spot = lax.broadcasted_iota(jnp.int32, (1, span), 1) + (count - 1) * span
        bias = jnp.where(spot < length, 0.0, -1e30)
        tree = []
        cached = []
        for g in range(groups):
            start = width + g * tile
            scores = dot(spread[g], triple_ref[:, start : start + tile], ((1,), (1,))) * scale
            tree.append(jnp.where(allowed, scores, -1e30))
            cached.append([])
        for c in range(count):
            copy(0, c).wait()
            for g in range(groups):
                lanes = slice(g * tile, (g + 1) * tile)
                keys = held[0, c * span : (c + 1) * span, lanes]
                scores = dot(spread[g], keys, ((1,), (1,))) * scale
                cached[g].append(scores + bias if c == count - 1 else scores)
        for c in range(count):
            copy(1, c).wait()
        for g in range(groups):
            lanes = slice(g * tile, (g + 1) * tile)
            start = 2 * width + g * tile
            peak = jnp.max(tree[g], axis=1, keepdims=True)
            most = cached[g][0]
            for scores in cached[g][1:]:
                most = jnp.maximum(most, scores)
            peak = jnp.maximum(peak, jnp.max(most, axis=1, keepdims=True))
            weights = [jnp.exp2(scores - peak) for scores in cached[g]]
            near = jnp.exp2(tree[g] - peak)
            total = weights[0]
            for more in weights[1:]:
                total = total + more
            total = jnp.sum(total, axis=1, keepdims=True) + jnp.sum(near, axis=1, keepdims=True)
            weights = jnp.concatenate([part.astype(BF16) for part in weights], axis=1)
            gathered = dot(weights, held[1, : count * span, lanes])
            gathered += dot(near.astype(BF16), triple_ref[:, start : start + tile])
            share = gathered / total
            out = jnp.zeros((NODES, tile), F32)
            for h in range(HEADS):
                out = jnp.where(head_of_lane == h, share[h * NODES : (h + 1) * NODES, :], out)
            out_ref[:, lanes] = out.astype(BF16)

    needed = (length + span - 1) // span
    for count in range(1, chunks + 1):
        @pl.when(needed == count)
        def run():
            attend_to(count)


def attend(j, lengths, triple, masks, chosen, cache, after=()):
    cache_span, width = cache.shape[2:]
    tile = HEADS * HEAD_SIZE
    groups = width // tile
    span = min(512, cache_span)
    chunks = cache_span // span
    depth = chosen.shape[1]
    return ordered(
        functools.partial(attend_kernel, j, span, groups),
        after,
        (lengths, triple, masks, chosen, cache),
        [
            pl.BlockSpec(memory_space=pltpu.SMEM),
            whole(triple.shape),
            whole(masks.shape),
            whole(chosen.shape),
            pl.BlockSpec(memory_space=pltpu.HBM),
        ],
        40,
        LARGE if j else SMALL,
        out_specs=[whole((NODES, width)), whole((2, depth, width))],
        out_shape=[
            jax.ShapeDtypeStruct((NODES, width), BF16),
            jax.ShapeDtypeStruct((2, depth, width), BF16),
        ],
        scratch_shapes=[
            pltpu.VMEM((groups, HEADS * NODES, tile), BF16),
            pltpu.VMEM((2, cache_span, width), BF16),
            pltpu.SemaphoreType.DMA((2, chunks)),
        ],
    )


def pack_kernel(*refs):
    rows = refs[0].shape[0]
    for i, ref in enumerate(refs[:-1]):
        refs[-1][i * rows : (i + 1) * rows, :] = ref[...]


def pack(pieces, after=()):
    rows, width = pieces[0].shape
    return ordered(
        pack_kernel,
        after,
        pieces,
        [whole((rows, width))] * len(pieces),
        16,
        out_shape=jax.ShapeDtypeStruct((rows * len(pieces), width), BF16),
    )


def lift_kernel(planes, slots, *refs):
    pieces = refs[:-4]
    weight_ref, own_ref, other_ref, rows = refs[-4:]
    share = rows.shape[0] // planes
    for k in range(planes):
        at = k * share
        for piece in pieces:
            for q in range(piece.shape[0] // (planes * slots)):
                rows[at : at + slots, :] = piece[
                    (q * planes + k) * slots : (q * planes + k + 1) * slots, :
                ]
                at += slots
    lifted = dot(weight_ref[...], rows[...], ((1,), (1,)))
    for k in range(planes):
        piece = lifted[:, k * share : (k + 1) * share]
        if k % 2 == 0:
            own_ref[k // 2] = piece
        else:
            other_ref[k // 2] = piece.astype(BF16)


def lift(pieces, planes, slots, weight, after=()):
    wide, width = weight.shape
    rows = sum(piece.shape[0] for piece in pieces)
    return ordered(
        functools.partial(lift_kernel, planes, slots),
        after,
        (*pieces, weight),
        [whole(piece.shape) for piece in pieces] + [whole(weight.shape)],
        20,
        out_shape=[
            jax.ShapeDtypeStruct((planes // 2, wide, rows // planes), F32),
            jax.ShapeDtypeStruct((planes // 2, wide, rows // planes), BF16),
        ],
        scratch_shapes=[pltpu.VMEM((rows, width), BF16)],
    )


def settle_kernel(own_ref, got_ref, kept_ref, send_ref, *_):
    kept_ref[...] = own_ref[0] + got_ref[0].astype(F32)
    send_ref[...] = (own_ref[1] + got_ref[1].astype(F32)).astype(BF16)


def settle(own, got, passed=()):
    shape = own.shape[1:]
    return ordered(
        settle_kernel,
        passed,
        (own, got),
        [whole(own.shape)] * 2,
        16,
        out_specs=[whole(shape)] * 2 + [pl.BlockSpec(memory_space=pl.ANY)] * len(passed),
        out_shape=[jax.ShapeDtypeStruct(shape, F32), jax.ShapeDtypeStruct(shape, BF16)]
        + [jax.ShapeDtypeStruct(array.shape, array.dtype) for array in passed],
        input_output_aliases={i: 2 + i for i in range(len(passed))},
    )


def final_kernel(place_ref, *refs):
    sums = [
        (refs[2 * j][...] + refs[2 * j + 1][...].astype(F32)).astype(BF16) for j in range(2)
    ]
    refs[-1][...] = dot(jnp.concatenate(sums, axis=1), place_ref[...]).astype(BF16)


def on_device(
    stream,
    row_tree_nodes,
    input_norm_gain,
    query_key_value_weight,
    adapter_down_weight,
    adapter_up_weight,
    key_value_cache,
    cache_length,
    parents,
    accepted,
    output_weight,
):
    rows, width_in = stream.shape
    planes = row_tree_nodes.shape[0] // rows
    owners = width_in // query_key_value_weight.shape[0]
    slots = rows // (2 * owners)
    columns = query_key_value_weight.shape[0]
    width = query_key_value_weight.shape[2]
    rank_rows = adapter_up_weight.shape[0]
    weight = jnp.swapaxes(query_key_value_weight, 0, 1)
    up = jnp.swapaxes(adapter_up_weight, 0, 1)
    down = jnp.swapaxes(output_weight, 0, 1)
    ids = row_tree_nodes.reshape(-1, LANES)

    def first_mask(h):
        return 2 if h % 2 == 0 else 4

    core_pairs = [(h, h ^ 1) for h in range(owners)]
    first_pairs = [(h, h ^ first_mask(h)) for h in range(owners)]
    second_pairs = [(h, h ^ (6 - first_mask(h))) for h in range(owners)]

    def across(array, k):
        return lax.ppermute(array, "tok", [(z, z ^ k) for z in range(planes)])

    weights = (weight, lax.ppermute(weight, "head", core_pairs))
    ups = (up, lax.ppermute(up, "head", core_pairs))
    feature, place = ordered(
        functools.partial(norm_kernel, slots, rank_rows),
        (),
        (ids, stream, input_norm_gain.reshape(-1, LANES), adapter_down_weight),
        [whole(ids.shape), pl.BlockSpec(memory_space=pltpu.HBM),
         whole((width_in // LANES, LANES)), pl.BlockSpec(memory_space=pltpu.HBM)],
        62,
        out_shape=[
            jax.ShapeDtypeStruct((rows // 2, 2 * columns + LANES), BF16),
            jax.ShapeDtypeStruct((rows, rows), BF16),
        ],
        scratch_shapes=[
            pltpu.VMEM((rows, width_in), BF16),
            pltpu.VMEM((rows, width_in), BF16),
            pltpu.VMEM(adapter_down_weight.shape, BF16),
            pltpu.SemaphoreType.DMA((rows // CHUNK,)),
            pltpu.SemaphoreType.DMA,
        ],
    )

    def swap(send, pairs, batch):
        return lax.ppermute(send.reshape(batch, -1, send.shape[-1]), "head", pairs)

    def split(keep, got, batch, after=()):
        return part(keep.reshape(batch, -1, keep.shape[-1]), got, 3, after)

    beyond, beside = across(feature, 2), across(feature, 1)
    own_keep, own_send = project([feature], weights, ups)
    own_got = swap(own_send, first_pairs, 2)
    depth = accepted.shape[1]
    masks, chosen = ordered(
        functools.partial(prep_kernel, slots, planes, rows),
        (own_send,),
        (ids, parents, accepted),
        [whole(ids.shape), whole(parents.shape), whole(accepted.shape)],
        16,
        out_shape=[
            jax.ShapeDtypeStruct((2, NODES, NODES), F32),
            jax.ShapeDtypeStruct((2, depth, NODES), F32),
        ],
    )
    onward = pass_on(beyond, (chosen, beside))
    furthest = across(onward, 1)
    mid_keep, mid_send = project([beside, onward], weights, ups)
    mid_got = swap(mid_send, first_pairs, 4)
    own_keep, *own_sends = split(own_keep, own_got, 2, (mid_send,))
    far_keep, far_send = project([furthest], weights, ups, (own_sends[1],))
    far_got = swap(far_send, first_pairs, 2)
    mid_keep, *mid_sends = split(mid_keep, mid_got, 4, (far_send,))
    far_keep, *far_sends = split(far_keep, far_got, 2, (mid_sends[1],))
    mid_sends[1] = pass_on(mid_sends[1], (far_sends[1],))
    keeps = (own_keep, mid_keep, far_keep)
    pairs = [
        [
            (keep, lax.ppermute(sends[j], "head", second_pairs))
            for keep, sends in zip(keeps, (own_sends, mid_sends, far_sends))
        ]
        for j in range(2)
    ]
    triple = join(0, pairs[0], 3)
    out0, kept0 = attend(0, cache_length, triple, masks, chosen, key_value_cache)

    def spread_out(out):
        away_first = lax.ppermute(out, "head", first_pairs)
        away_second = lax.ppermute(out, "head", second_pairs)
        away_both = lax.ppermute(out, "head", [(h, h ^ 6) for h in range(owners)])
        return (out, away_second, away_first, away_both)

    side0 = spread_out(out0)
    triple = join(1, pairs[1], 3, (out0,))
    out1, kept1 = attend(1, cache_length, triple, masks, chosen, key_value_cache)
    side1 = spread_out(out1)

    def other_core(packed):
        return packed, lax.ppermute(packed, "head", core_pairs)

    own0, away0 = lift(other_core(pack(side0, (out1,))), planes, slots, down)
    home0 = across(away0, 1)
    own0, away0, packed = settle(own0, home0, (pack(side1, (own0,)),))
    home0 = across(away0, 2)
    own1, away1 = lift(other_core(packed), planes, slots, down)
    own1, away1 = settle(own1, across(away1, 1))
    home1 = across(away1, 2)
    operands = (place, own0, home0, own1, home1)
    attended = ordered(
        final_kernel,
        (),
        operands,
        [whole(operand.shape) for operand in operands],
        16,
        out_shape=jax.ShapeDtypeStruct((output_weight.shape[1], rows), BF16),
    )
    return jnp.swapaxes(attended, 0, 1), jnp.stack([kept0, kept1], axis=1)


def ancestors_of(parents):
    parent_links = jax.nn.one_hot(parents, NODES, dtype=jnp.float32)
    identity_matrix = jnp.eye(NODES, dtype=jnp.float32)
    ancestry = jnp.minimum(identity_matrix[None] + parent_links, 1.0)
    for squaring in range(NODES.bit_length()):
        ancestry = jnp.minimum(
            jnp.einsum("rnm,rmk->rnk", ancestry, ancestry, precision=lax.Precision.HIGHEST), 1.0
        )
    return ancestry


def plain_on_device(
    stream,
    row_tree_nodes,
    input_norm_gain,
    query_key_value_weight,
    adapter_down_weight,
    adapter_up_weight,
    key_value_cache,
    cache_length,
    parents,
    accepted,
    output_weight,
):
    owner_index = lax.axis_index("head")
    feature_rows = query_key_value_weight.shape[0]
    device_width = query_key_value_weight.shape[2]
    adapter_rank_rows = adapter_up_weight.shape[0]
    local_heads = device_width // HEAD_SIZE
    request_count = key_value_cache.shape[1]
    cache_span = key_value_cache.shape[2]
    wide_rows = stream.astype(jnp.float32)
    inverse_rms = lax.rsqrt(jnp.mean(wide_rows * wide_rows, axis=1, keepdims=True) + 1e-05)
    normalized_input = (wide_rows * inverse_rms * input_norm_gain.astype(jnp.float32)).astype(
        jnp.bfloat16
    )
    reduced_rank_rows = jnp.dot(
        normalized_input, adapter_down_weight, preferred_element_type=jnp.float32
    ).astype(jnp.bfloat16)
    feature_block = lax.dynamic_slice_in_dim(
        normalized_input, owner_index * feature_rows, feature_rows, 1
    )
    rank_block = lax.dynamic_slice_in_dim(
        reduced_rank_rows, owner_index * adapter_rank_rows, adapter_rank_rows, 1
    )
    gathered_features, gathered_ranks = (
        lax.all_gather(feature_block, "tok", axis=0, tiled=True),
        lax.all_gather(rank_block, "tok", axis=0, tiled=True),
    )
    projection = query_key_value_weight.reshape(feature_rows, 3 * device_width)
    lifting_matrix = adapter_up_weight.reshape(adapter_rank_rows, 3 * device_width)
    node_to_row = jnp.argsort(row_tree_nodes)
    part_sum = jnp.dot(
        gathered_features[node_to_row], projection, preferred_element_type=jnp.float32
    )
    node_rows = lax.psum_scatter(
        part_sum
        + jnp.dot(gathered_ranks[node_to_row], lifting_matrix, preferred_element_type=jnp.float32),
        "head",
        scatter_dimension=0,
        tiled=True,
    ).astype(jnp.bfloat16)
    triple = node_rows.reshape(request_count, NODES, 3, local_heads, HEAD_SIZE)
    queries = triple[:, :, 0]
    tree_key_rows = triple[:, :, 1]
    tree_value_rows = triple[:, :, 2]
    ancestry = ancestors_of(parents)
    attention_score_scale = HEAD_SIZE ** (-0.5)
    tree_score_matrix = (
        jnp.einsum("rnhd,rmhd->rhnm", queries, tree_key_rows, preferred_element_type=jnp.float32)
        * attention_score_scale
    )
    tree_score_matrix = jnp.where(ancestry[:, None] > 0.5, tree_score_matrix, -jnp.inf)
    keys_cache = key_value_cache[0].reshape(request_count, cache_span, local_heads, HEAD_SIZE)
    values_cache = key_value_cache[1].reshape(request_count, cache_span, local_heads, HEAD_SIZE)
    scores = (
        jnp.einsum("rnhd,rchd->rhnc", queries, keys_cache, preferred_element_type=jnp.float32)
        * attention_score_scale
    )
    positions = lax.broadcasted_iota(jnp.int32, (1, 1, 1, cache_span), 3)
    scores = jnp.where(positions < cache_length[:, None, None, None], scores, -jnp.inf)
    tree_top = jnp.max(tree_score_matrix, axis=-1, keepdims=True)
    largest = jnp.maximum(tree_top, jnp.max(scores, axis=-1, keepdims=True))
    cache_exp = jnp.exp(scores - largest)
    tree_exp = jnp.exp(tree_score_matrix - largest)
    totals = jnp.sum(cache_exp, axis=-1, keepdims=True) + jnp.sum(tree_exp, axis=-1, keepdims=True)
    cache_weights = (cache_exp / totals).astype(jnp.bfloat16)
    tree_weight_matrix = (tree_exp / totals).astype(jnp.bfloat16)
    attention = jnp.einsum(
        "rhnc,rchd->rnhd", cache_weights, values_cache, preferred_element_type=jnp.float32
    )
    attention = attention + jnp.einsum(
        "rhnm,rmhd->rnhd", tree_weight_matrix, tree_value_rows, preferred_element_type=jnp.float32
    )
    head_rows = attention.astype(jnp.bfloat16).reshape(request_count * NODES, device_width)
    node_table = node_rows.reshape(request_count, NODES, 3, device_width)
    chosen = jnp.take_along_axis(node_table, accepted[:, :, None, None], axis=1)
    accepted_kv = jnp.stack([chosen[:, :, 1], chosen[:, :, 2]])
    everything = lax.all_gather(head_rows, "head", axis=0, tiled=True)
    attended = lax.psum_scatter(
        jnp.dot(
            everything[row_tree_nodes], output_weight, preferred_element_type=jnp.float32
        ).astype(jnp.bfloat16),
        "tok",
        scatter_dimension=0,
        tiled=True,
    )
    return (attended, accepted_kv)


def solution(mesh):
    placed = (
        P("tok", None),
        P(),
        P(),
        P("head", None, "tok"),
        P(),
        P("head", None, "tok"),
        P(None, "head", None, "tok"),
        P("head"),
        P("head", None),
        P("head", None),
        P("tok", "head"),
    )
    sized = mesh.shape["head"] == 8 and mesh.shape["tok"] == 4
    return jax.shard_map(
        on_device if sized else plain_on_device,
        mesh=mesh,
        in_specs=placed,
        out_specs=(P("tok", "head"), P(None, "head", None, "tok")),
        check_vma=False,
    )
```

```python
import functools

import jax
import jax.numpy as jnp
from jax import lax
from jax.experimental import pallas as pl
from jax.experimental.pallas import tpu as pltpu
from jax.sharding import PartitionSpec as P

HEAD_SIZE = 224
NODES = 64
LANES = 128
F32 = jnp.float32
BF16 = jnp.bfloat16
TOKEN = jax.ShapeDtypeStruct((8, 128), F32)
SMALL = pl.CostEstimate(flops=1, bytes_accessed=1, transcendentals=0)
LARGE = pl.CostEstimate(flops=2 * 10**11, bytes_accessed=1, transcendentals=0)


def dot(a, b, dims=((1,), (0,))):
    return lax.dot_general(a, b, (dims, ((), ())), preferred_element_type=F32)


def whole(shape):
    return pl.BlockSpec(shape, lambda *_: (0,) * len(shape))


def ordered(kernel, after, operands, in_specs, megabytes, cost=SMALL, **options):
    count = len(after)

    def body(*refs):
        kernel(*refs[count:])

    return pl.pallas_call(
        body,
        in_specs=[pl.BlockSpec(memory_space=pl.ANY)] * count + in_specs,
        compiler_params=pltpu.CompilerParams(vmem_limit_bytes=megabytes * 2**20),
        cost_estimate=cost,
        **options,
    )(*after, *operands)


def row_to_column(row):
    size = row.shape[1]
    eye = lax.broadcasted_iota(jnp.int32, (size, size), 0) == lax.broadcasted_iota(
        jnp.int32, (size, size), 1
    )
    return jnp.sum(jnp.where(eye, row, 0), axis=1, keepdims=True)


def rank_in_plane(row):
    before = row_to_column(row) < row
    return jnp.sum(before.astype(jnp.int32), axis=0, keepdims=True)


def plane_row(ids_ref, plane, rows):
    per = rows // LANES
    parts = [ids_ref[pl.ds(plane * per + i, 1), :] for i in range(per)]
    return jnp.concatenate(parts, axis=1)


CHUNK = 32


def norm_kernel(slots, rank_rows, ids_ref, stream_hbm, gain_ref, down_hbm, feature_ref,
                place_ref, normed, held, down_ref, arrived, down_arrived):
    me = lax.axis_index("head")
    plane = lax.axis_index("tok")
    rows, width = held.shape
    copies = [
        pltpu.make_async_copy(
            stream_hbm.at[pl.ds(i * CHUNK, CHUNK), :],
            held.at[pl.ds(i * CHUNK, CHUNK), :],
            arrived.at[i],
        )
        for i in range(rows // CHUNK)
    ]
    for copy in copies:
        copy.start()
    down_copy = pltpu.make_async_copy(down_hbm, down_ref, down_arrived)
    down_copy.start()
    gains = gain_ref[...].astype(F32)
    gain = jnp.concatenate([gains[i : i + 1] for i in range(width // LANES)], axis=1)

    def norm(i, carry):
        at = pl.ds(pl.multiple_of(i * CHUNK, CHUNK), CHUNK)
        pltpu.make_async_copy(stream_hbm.at[at, :], held.at[at, :], arrived.at[i]).wait()
        wide = held[at, :].astype(F32)
        rstd = lax.rsqrt(jnp.sum(wide * wide, axis=1, keepdims=True) / width + 1e-05)
        normed[at, :] = (wide * rstd * gain).astype(BF16)
        return carry

    lax.fori_loop(0, rows // CHUNK, norm, 0)
    down_copy.wait()
    low = dot(normed[...], down_ref[...]).astype(BF16)
    ranks = low.shape[1]
    lane = lax.broadcasted_iota(jnp.int32, (ranks, LANES), 1)
    wanted = jnp.where(lane < rank_rows, me * rank_rows + lane, (me ^ 1) * rank_rows + lane - rank_rows)
    pick = lax.broadcasted_iota(jnp.int32, (ranks, LANES), 0) == wanted
    pick &= lane < 2 * rank_rows
    low = dot(low, pick.astype(BF16)).astype(BF16)
    ids = plane_row(ids_ref, plane, rows)
    rank = rank_in_plane(ids)
    owner = ids // (2 * NODES)
    second = (ids // NODES) % 2
    apart = owner ^ me
    even = (owner & 1) == 0
    bit_x = (apart >> 1) & 1
    bit_y = (apart >> 2) & 1
    order = (apart & 1) * 4 + jnp.where(even, bit_x * 2 + bit_y, bit_y * 2 + bit_x)
    half = rows // 2
    position = second * half + order * slots + rank % slots
    place_ref[...] = (
        lax.broadcasted_iota(jnp.int32, (rows, rows), 0) == position
    ).astype(BF16)
    quarter = half // 2
    position = jnp.where(order < 4, second * quarter + order * slots + rank % slots, -1)
    place = (lax.broadcasted_iota(jnp.int32, (half, rows), 0) == position).astype(BF16)
    columns = (feature_ref.shape[1] - LANES) // 2
    for i, owner_of in enumerate((me, me ^ 1)):
        block = normed[:, pl.ds(pl.multiple_of(owner_of * columns, LANES), columns)]
        feature_ref[:, i * columns : (i + 1) * columns] = dot(place, block).astype(BF16)
    feature_ref[:, 2 * columns :] = dot(place, low).astype(BF16)


def prep_kernel(slots, planes, rows, ids_ref, parents_ref, accepted_ref, mask_ref, chosen_ref):
    me = lax.axis_index("head")
    plane = lax.axis_index("tok")
    for j in range(2):
        nodes = []
        for k in range(planes):
            ids = plane_row(ids_ref, plane ^ k, rows)
            rank = rank_in_plane(ids)
            spot = lax.broadcasted_iota(jnp.int32, (slots, rows), 0) + (me * 2 + j) * slots
            nodes.append(
                jnp.sum(jnp.where(rank == spot, ids, 0), axis=1, keepdims=True)
                - (me * 2 + j) * NODES
            )
        nodes = jnp.concatenate(nodes, axis=0)
        lanes = lax.broadcasted_iota(jnp.int32, (NODES, NODES), 1)
        rows_of = lax.broadcasted_iota(jnp.int32, (NODES, NODES), 0)
        named = (nodes == lanes).astype(BF16)
        parent = row_to_column(parents_ref[j : j + 1, :])
        reach = ((parent == lanes) | (rows_of == lanes)).astype(BF16)
        for _ in range((NODES - 1).bit_length()):
            reach = jnp.minimum(dot(reach, reach), 1.0).astype(BF16)
        mask_ref[j] = dot(dot(named, reach).astype(BF16), named, ((1,), (1,)))
        accepted = row_to_column(accepted_ref[j : j + 1, :])
        depth = accepted.shape[0]
        wanted = (accepted == lax.broadcasted_iota(jnp.int32, (depth, NODES), 1)).astype(BF16)
        chosen_ref[j] = dot(wanted, named, ((1,), (1,)))


def tiles_of(width):
    first = (width // 512 + 1) * 256 if width % 512 else width // 2
    return [(0, first), (first, width - first)]


def project_kernel(pieces, *refs):
    lhs_refs = refs[:pieces]
    weight_refs = refs[pieces : pieces + 2]
    up_refs = refs[pieces + 2 : pieces + 4]
    keep_hbm, send_hbm, token_ref = refs[pieces + 4 : pieces + 7]
    token_ref[...] = jnp.zeros(token_ref.shape, F32)
    lhs, held, keep, send, arrived, left = refs[-6:]
    parts, columns, width = weight_refs[0].shape
    deep = held.shape[1]
    half = lhs.shape[0] // 2
    rank_rows = up_refs[0].shape[1]
    steps = [(p, start, size) for p in range(parts) for start, size in tiles_of(width)]

    def inward(i, side):
        p, start, size = steps[i]
        return pltpu.make_async_copy(
            weight_refs[side].at[p, :, pl.ds(start, size)],
            held.at[p, pl.ds(side * columns, columns), pl.ds(start, size)],
            arrived.at[i, side],
        )

    for i in range(len(steps)):
        for side in range(2):
            inward(i, side).start()
    at = 0
    for lhs_ref in lhs_refs:
        rows = lhs_ref.shape[0] // 4
        for j in range(2):
            lhs[at : at + rows, :] = lhs_ref[2 * j * rows : (2 * j + 1) * rows, :]
            lhs[half + at : half + at + rows, :] = lhs_ref[
                (2 * j + 1) * rows : (2 * j + 2) * rows, :
            ]
            at += rows
    for p in range(parts):
        low = 2 * columns
        for side in range(2):
            held[p, low : low + rank_rows, :] = up_refs[side][p]
            low += rank_rows
        held[p, low:, :] = jnp.zeros((deep - low, width), BF16)
    outward = []
    for i, (p, start, size) in enumerate(steps):
        for side in range(2):
            inward(i, side).wait()
        lanes = slice(p * width + start, p * width + start + size)
        total = dot(lhs[...], held[p, :, start : start + size])
        keep[:, lanes] = total[:half]
        send[:, lanes] = total[half:].astype(BF16)
        for j, (source, target) in enumerate(((keep, keep_hbm), (send, send_hbm))):
            copy = pltpu.make_async_copy(source.at[:, lanes], target.at[:, lanes], left.at[i, j])
            copy.start()
            outward.append(copy)
    for copy in outward:
        copy.wait()


def project(pieces, weights, ups, after=()):
    parts, columns, width = weights[0].shape
    steps = parts * len(tiles_of(width))
    rows = sum(piece.shape[0] for piece in pieces) // 2
    deep = pieces[0].shape[1]
    far = pl.BlockSpec(memory_space=pltpu.HBM)
    return ordered(
        functools.partial(project_kernel, len(pieces)),
        after,
        (*pieces, *weights, *ups),
        [whole(piece.shape) for piece in pieces] + [far] * 2 + [whole(ups[0].shape)] * 2,
        55,
        LARGE,
        out_specs=[far] * 2 + [whole(TOKEN.shape)],
        out_shape=[
            jax.ShapeDtypeStruct((rows, parts * width), F32),
            jax.ShapeDtypeStruct((rows, parts * width), BF16),
            TOKEN,
        ],
        scratch_shapes=[
            pltpu.VMEM((2 * rows, deep), BF16),
            pltpu.VMEM((parts, deep, width), BF16),
            pltpu.VMEM((rows, parts * width), F32),
            pltpu.VMEM((rows, parts * width), BF16),
            pltpu.SemaphoreType.DMA((steps, 2)),
            pltpu.SemaphoreType.DMA((steps, 2)),
        ],
    )


def pass_kernel(*refs):
    pass


def pass_on(array, after):
    return ordered(
        pass_kernel,
        (*after, array),
        (),
        [],
        16,
        out_specs=pl.BlockSpec(memory_space=pl.ANY),
        out_shape=jax.ShapeDtypeStruct(array.shape, array.dtype),
        input_output_aliases={len(after): 0},
    )


def part_kernel(keep_ref, got_ref, kept_ref, token_ref, *send_refs):
    token_ref[...] = jnp.zeros(token_ref.shape, F32)
    added = keep_ref[...] + got_ref[...].astype(F32)
    half = added.shape[1] // 2
    kept_ref[...] = added[:, :half]
    for b in range(added.shape[0]):
        send_refs[b % 2][b // 2] = added[b, half:].astype(BF16)


def part(keep, got, parts, after=()):
    batch, rows, wide = keep.shape
    tile = wide // parts
    half = rows // 2

    def block(batch, rows):
        return pl.BlockSpec((batch, rows, tile), lambda c: (0, 0, c))

    return ordered(
        part_kernel,
        after,
        (keep, got),
        [block(batch, rows)] * 2,
        16,
        grid=(parts,),
        out_specs=[block(batch, half), whole(TOKEN.shape)] + [block(batch // 2, half)] * 2,
        out_shape=[jax.ShapeDtypeStruct((batch, half, wide), F32), TOKEN]
        + [jax.ShapeDtypeStruct((batch // 2, half, wide), BF16)] * 2,
    )


def join_kernel(*refs):
    out_ref = refs[-1]
    slots = refs[0].shape[-2]
    at = 0
    for keep_ref, got_ref in zip(refs[:-1:2], refs[1:-1:2]):
        for k in range(keep_ref.shape[0]):
            out_ref[at : at + slots] = (keep_ref[k] + got_ref[k].astype(F32)).astype(BF16)
            at += slots


def join(j, pairs, parts, after=()):
    slots, wide = pairs[0][0].shape[1:]
    tile = wide // parts
    specs = []
    operands = []
    for keep, got in pairs:
        planes = got.shape[0]
        specs.append(pl.BlockSpec((planes, None, slots, tile), lambda c: (0, j, 0, c)))
        specs.append(pl.BlockSpec((planes, slots, tile), lambda c: (0, 0, c)))
        operands += [keep.reshape(planes, 2, slots, wide), got]
    rows = sum(pair[1].shape[0] for pair in pairs) * slots
    return ordered(
        join_kernel,
        after,
        operands,
        specs,
        16,
        grid=(parts,),
        out_specs=pl.BlockSpec((rows, tile), lambda c: (0, c)),
        out_shape=jax.ShapeDtypeStruct((rows, wide), BF16),
    )


HEADS = 4
LOG2E = 1.4426950408889634


def attend_kernel(j, span, groups, length_ref, triple_ref, mask_ref, chosen_ref, cache_ref,
                  out_ref, kept_ref, spread, held, arrived):
    chunks = held.shape[1] // span
    tile = spread.shape[2]
    width = groups * tile
    length = length_ref[j]
    scale = HEAD_SIZE ** (-0.5) * LOG2E

    def copy(part, c):
        at = pl.ds(c * span, span)
        return pltpu.make_async_copy(
            cache_ref.at[part, j, at, :], held.at[part, at, :], arrived.at[part, c]
        )

    for part in range(2):
        for c in range(chunks):
            copy(part, c).start()

    head_of_lane = lax.broadcasted_iota(jnp.int32, (1, tile), 1) // HEAD_SIZE
    pick = chosen_ref[j].astype(BF16)
    for g in range(groups):
        lanes = slice(g * tile, (g + 1) * tile)
        query = triple_ref[:, lanes]
        for h in range(HEADS):
            spread[g, h * NODES : (h + 1) * NODES, :] = jnp.where(head_of_lane == h, query, 0)
        for part in range(2):
            start = (part + 1) * width + g * tile
            kept_ref[part, :, lanes] = dot(pick, triple_ref[:, start : start + tile]).astype(BF16)

    allowed = jnp.concatenate([mask_ref[j]] * HEADS, axis=0) > 0.5
    tree = []
    cached = []
    for g in range(groups):
        start = width + g * tile
        scores = dot(spread[g], triple_ref[:, start : start + tile], ((1,), (1,))) * scale
        tree.append(jnp.where(allowed, scores, -1e30))
        cached.append([])
    for c in range(chunks):
        copy(0, c).wait()
        spot = lax.broadcasted_iota(jnp.int32, (1, span), 1) + c * span
        bias = jnp.where(spot < length, 0.0, -1e30)
        for g in range(groups):
            lanes = slice(g * tile, (g + 1) * tile)
            keys = held[0, c * span : (c + 1) * span, lanes]
            scores = dot(spread[g], keys, ((1,), (1,))) * scale
            cached[g].append(scores + bias)
    for c in range(chunks):
        copy(1, c).wait()
    for g in range(groups):
        lanes = slice(g * tile, (g + 1) * tile)
        start = 2 * width + g * tile
        peak = jnp.max(tree[g], axis=1, keepdims=True)
        most = cached[g][0]
        for scores in cached[g][1:]:
            most = jnp.maximum(most, scores)
        peak = jnp.maximum(peak, jnp.max(most, axis=1, keepdims=True))
        weights = [jnp.exp2(scores - peak) for scores in cached[g]]
        near = jnp.exp2(tree[g] - peak)
        total = weights[0]
        for more in weights[1:]:
            total = total + more
        total = jnp.sum(total, axis=1, keepdims=True) + jnp.sum(near, axis=1, keepdims=True)
        weights = jnp.concatenate([part.astype(BF16) for part in weights], axis=1)
        gathered = dot(weights, held[1, :, lanes])
        gathered += dot(near.astype(BF16), triple_ref[:, start : start + tile])
        share = gathered / total
        out = jnp.zeros((NODES, tile), F32)
        for h in range(HEADS):
            out = jnp.where(head_of_lane == h, share[h * NODES : (h + 1) * NODES, :], out)
        out_ref[:, lanes] = out.astype(BF16)


def attend(j, lengths, triple, masks, chosen, cache, after=()):
    cache_span, width = cache.shape[2:]
    tile = HEADS * HEAD_SIZE
    groups = width // tile
    span = min(512, cache_span)
    chunks = cache_span // span
    depth = chosen.shape[1]
    return ordered(
        functools.partial(attend_kernel, j, span, groups),
        after,
        (lengths, triple, masks, chosen, cache),
        [
            pl.BlockSpec(memory_space=pltpu.SMEM),
            whole(triple.shape),
            whole(masks.shape),
            whole(chosen.shape),
            pl.BlockSpec(memory_space=pltpu.HBM),
        ],
        40,
        LARGE if j else SMALL,
        out_specs=[whole((NODES, width)), whole((2, depth, width))],
        out_shape=[
            jax.ShapeDtypeStruct((NODES, width), BF16),
            jax.ShapeDtypeStruct((2, depth, width), BF16),
        ],
        scratch_shapes=[
            pltpu.VMEM((groups, HEADS * NODES, tile), BF16),
            pltpu.VMEM((2, cache_span, width), BF16),
            pltpu.SemaphoreType.DMA((2, chunks)),
        ],
    )


def pack_kernel(*refs):
    rows = refs[0].shape[0]
    for i, ref in enumerate(refs[:-1]):
        refs[-1][i * rows : (i + 1) * rows, :] = ref[...]


def pack(pieces, after=()):
    rows, width = pieces[0].shape
    return ordered(
        pack_kernel,
        after,
        pieces,
        [whole((rows, width))] * len(pieces),
        16,
        out_shape=jax.ShapeDtypeStruct((rows * len(pieces), width), BF16),
    )


def lift_kernel(planes, slots, *refs):
    pieces = refs[:-4]
    weight_ref, own_ref, other_ref, rows = refs[-4:]
    share = rows.shape[0] // planes
    for k in range(planes):
        at = k * share
        for piece in pieces:
            for q in range(piece.shape[0] // (planes * slots)):
                rows[at : at + slots, :] = piece[
                    (q * planes + k) * slots : (q * planes + k + 1) * slots, :
                ]
                at += slots
    lifted = dot(weight_ref[...], rows[...], ((1,), (1,)))
    for k in range(planes):
        piece = lifted[:, k * share : (k + 1) * share]
        if k % 2 == 0:
            own_ref[k // 2] = piece
        else:
            other_ref[k // 2] = piece.astype(BF16)


def lift(pieces, planes, slots, weight, after=()):
    wide, width = weight.shape
    rows = sum(piece.shape[0] for piece in pieces)
    return ordered(
        functools.partial(lift_kernel, planes, slots),
        after,
        (*pieces, weight),
        [whole(piece.shape) for piece in pieces] + [whole(weight.shape)],
        20,
        out_shape=[
            jax.ShapeDtypeStruct((planes // 2, wide, rows // planes), F32),
            jax.ShapeDtypeStruct((planes // 2, wide, rows // planes), BF16),
        ],
        scratch_shapes=[pltpu.VMEM((rows, width), BF16)],
    )


def settle_kernel(own_ref, got_ref, kept_ref, send_ref, *_):
    kept_ref[...] = own_ref[0] + got_ref[0].astype(F32)
    send_ref[...] = (own_ref[1] + got_ref[1].astype(F32)).astype(BF16)


def settle(own, got, passed=()):
    shape = own.shape[1:]
    return ordered(
        settle_kernel,
        passed,
        (own, got),
        [whole(own.shape)] * 2,
        16,
        out_specs=[whole(shape)] * 2 + [pl.BlockSpec(memory_space=pl.ANY)] * len(passed),
        out_shape=[jax.ShapeDtypeStruct(shape, F32), jax.ShapeDtypeStruct(shape, BF16)]
        + [jax.ShapeDtypeStruct(array.shape, array.dtype) for array in passed],
        input_output_aliases={i: 2 + i for i in range(len(passed))},
    )


def final_kernel(place_ref, *refs):
    sums = [
        (refs[2 * j][...] + refs[2 * j + 1][...].astype(F32)).astype(BF16) for j in range(2)
    ]
    refs[-1][...] = dot(jnp.concatenate(sums, axis=1), place_ref[...]).astype(BF16)


def on_device(
    stream,
    row_tree_nodes,
    input_norm_gain,
    query_key_value_weight,
    adapter_down_weight,
    adapter_up_weight,
    key_value_cache,
    cache_length,
    parents,
    accepted,
    output_weight,
):
    rows, width_in = stream.shape
    planes = row_tree_nodes.shape[0] // rows
    owners = width_in // query_key_value_weight.shape[0]
    slots = rows // (2 * owners)
    columns = query_key_value_weight.shape[0]
    width = query_key_value_weight.shape[2]
    rank_rows = adapter_up_weight.shape[0]
    weight = jnp.swapaxes(query_key_value_weight, 0, 1)
    up = jnp.swapaxes(adapter_up_weight, 0, 1)
    down = jnp.swapaxes(output_weight, 0, 1)
    ids = row_tree_nodes.reshape(-1, LANES)

    def first_mask(h):
        return 2 if h % 2 == 0 else 4

    core_pairs = [(h, h ^ 1) for h in range(owners)]
    first_pairs = [(h, h ^ first_mask(h)) for h in range(owners)]
    second_pairs = [(h, h ^ (6 - first_mask(h))) for h in range(owners)]

    def across(array, k):
        return lax.ppermute(array, "tok", [(z, z ^ k) for z in range(planes)])

    weights = (weight, lax.ppermute(weight, "head", core_pairs))
    ups = (up, lax.ppermute(up, "head", core_pairs))
    feature, place = ordered(
        functools.partial(norm_kernel, slots, rank_rows),
        (),
        (ids, stream, input_norm_gain.reshape(-1, LANES), adapter_down_weight),
        [whole(ids.shape), pl.BlockSpec(memory_space=pltpu.HBM),
         whole((width_in // LANES, LANES)), pl.BlockSpec(memory_space=pltpu.HBM)],
        62,
        out_shape=[
            jax.ShapeDtypeStruct((rows // 2, 2 * columns + LANES), BF16),
            jax.ShapeDtypeStruct((rows, rows), BF16),
        ],
        scratch_shapes=[
            pltpu.VMEM((rows, width_in), BF16),
            pltpu.VMEM((rows, width_in), BF16),
            pltpu.VMEM(adapter_down_weight.shape, BF16),
            pltpu.SemaphoreType.DMA((rows // CHUNK,)),
            pltpu.SemaphoreType.DMA,
        ],
    )

    def swap(send, pairs, batch):
        return lax.ppermute(send.reshape(batch, -1, send.shape[-1]), "head", pairs)

    def split(keep, got, batch, after=()):
        return part(keep.reshape(batch, -1, keep.shape[-1]), got, 3, after)

    beyond, beside = across(feature, 2), across(feature, 1)
    own_keep, own_send, token = project([feature], weights, ups)
    own_got = swap(own_send, first_pairs, 2)
    depth = accepted.shape[1]
    masks, chosen = ordered(
        functools.partial(prep_kernel, slots, planes, rows),
        (token,),
        (ids, parents, accepted),
        [whole(ids.shape), whole(parents.shape), whole(accepted.shape)],
        16,
        out_shape=[
            jax.ShapeDtypeStruct((2, NODES, NODES), F32),
            jax.ShapeDtypeStruct((2, depth, NODES), F32),
        ],
    )
    onward = pass_on(beyond, (chosen, beside))
    furthest = across(onward, 1)
    mid_keep, mid_send, token = project([beside, onward], weights, ups)
    mid_got = swap(mid_send, first_pairs, 4)
    own_keep, token, *own_sends = split(own_keep, own_got, 2, (token,))
    far_keep, far_send, token = project([furthest], weights, ups, (token,))
    far_got = swap(far_send, first_pairs, 2)
    mid_keep, token, *mid_sends = split(mid_keep, mid_got, 4, (token,))
    far_keep, token, *far_sends = split(far_keep, far_got, 2, (token,))
    mid_sends[1] = pass_on(mid_sends[1], (token,))
    keeps = (own_keep, mid_keep, far_keep)
    pairs = [
        [
            (keep, lax.ppermute(sends[j], "head", second_pairs))
            for keep, sends in zip(keeps, (own_sends, mid_sends, far_sends))
        ]
        for j in range(2)
    ]
    triple = join(0, pairs[0], 3)
    out0, kept0 = attend(0, cache_length, triple, masks, chosen, key_value_cache)

    def spread_out(out):
        away_first = lax.ppermute(out, "head", first_pairs)
        away_second = lax.ppermute(out, "head", second_pairs)
        away_both = lax.ppermute(out, "head", [(h, h ^ 6) for h in range(owners)])
        return (out, away_second, away_first, away_both)

    side0 = spread_out(out0)
    triple = join(1, pairs[1], 3, (out0,))
    out1, kept1 = attend(1, cache_length, triple, masks, chosen, key_value_cache)
    side1 = spread_out(out1)

    def other_core(packed):
        return packed, lax.ppermute(packed, "head", core_pairs)

    own0, away0 = lift(other_core(pack(side0, (out1,))), planes, slots, down)
    home0 = across(away0, 1)
    own0, away0, packed = settle(own0, home0, (pack(side1, (own0,)),))
    home0 = across(away0, 2)
    own1, away1 = lift(other_core(packed), planes, slots, down)
    own1, away1 = settle(own1, across(away1, 1))
    home1 = across(away1, 2)
    operands = (place, own0, home0, own1, home1)
    attended = ordered(
        final_kernel,
        (),
        operands,
        [whole(operand.shape) for operand in operands],
        16,
        out_shape=jax.ShapeDtypeStruct((output_weight.shape[1], rows), BF16),
    )
    return jnp.swapaxes(attended, 0, 1), jnp.stack([kept0, kept1], axis=1)


def ancestors_of(parents):
    parent_links = jax.nn.one_hot(parents, NODES, dtype=jnp.float32)
    identity_matrix = jnp.eye(NODES, dtype=jnp.float32)
    ancestry = jnp.minimum(identity_matrix[None] + parent_links, 1.0)
    for squaring in range(NODES.bit_length()):
        ancestry = jnp.minimum(
            jnp.einsum("rnm,rmk->rnk", ancestry, ancestry, precision=lax.Precision.HIGHEST), 1.0
        )
    return ancestry


def plain_on_device(
    stream,
    row_tree_nodes,
    input_norm_gain,
    query_key_value_weight,
    adapter_down_weight,
    adapter_up_weight,
    key_value_cache,
    cache_length,
    parents,
    accepted,
    output_weight,
):
    owner_index = lax.axis_index("head")
    feature_rows = query_key_value_weight.shape[0]
    device_width = query_key_value_weight.shape[2]
    adapter_rank_rows = adapter_up_weight.shape[0]
    local_heads = device_width // HEAD_SIZE
    request_count = key_value_cache.shape[1]
    cache_span = key_value_cache.shape[2]
    wide_rows = stream.astype(jnp.float32)
    inverse_rms = lax.rsqrt(jnp.mean(wide_rows * wide_rows, axis=1, keepdims=True) + 1e-05)
    normalized_input = (wide_rows * inverse_rms * input_norm_gain.astype(jnp.float32)).astype(
        jnp.bfloat16
    )
    reduced_rank_rows = jnp.dot(
        normalized_input, adapter_down_weight, preferred_element_type=jnp.float32
    ).astype(jnp.bfloat16)
    feature_block = lax.dynamic_slice_in_dim(
        normalized_input, owner_index * feature_rows, feature_rows, 1
    )
    rank_block = lax.dynamic_slice_in_dim(
        reduced_rank_rows, owner_index * adapter_rank_rows, adapter_rank_rows, 1
    )
    gathered_features, gathered_ranks = (
        lax.all_gather(feature_block, "tok", axis=0, tiled=True),
        lax.all_gather(rank_block, "tok", axis=0, tiled=True),
    )
    projection = query_key_value_weight.reshape(feature_rows, 3 * device_width)
    lifting_matrix = adapter_up_weight.reshape(adapter_rank_rows, 3 * device_width)
    node_to_row = jnp.argsort(row_tree_nodes)
    part_sum = jnp.dot(
        gathered_features[node_to_row], projection, preferred_element_type=jnp.float32
    )
    node_rows = lax.psum_scatter(
        part_sum
        + jnp.dot(gathered_ranks[node_to_row], lifting_matrix, preferred_element_type=jnp.float32),
        "head",
        scatter_dimension=0,
        tiled=True,
    ).astype(jnp.bfloat16)
    triple = node_rows.reshape(request_count, NODES, 3, local_heads, HEAD_SIZE)
    queries = triple[:, :, 0]
    tree_key_rows = triple[:, :, 1]
    tree_value_rows = triple[:, :, 2]
    ancestry = ancestors_of(parents)
    attention_score_scale = HEAD_SIZE ** (-0.5)
    tree_score_matrix = (
        jnp.einsum("rnhd,rmhd->rhnm", queries, tree_key_rows, preferred_element_type=jnp.float32)
        * attention_score_scale
    )
    tree_score_matrix = jnp.where(ancestry[:, None] > 0.5, tree_score_matrix, -jnp.inf)
    keys_cache = key_value_cache[0].reshape(request_count, cache_span, local_heads, HEAD_SIZE)
    values_cache = key_value_cache[1].reshape(request_count, cache_span, local_heads, HEAD_SIZE)
    scores = (
        jnp.einsum("rnhd,rchd->rhnc", queries, keys_cache, preferred_element_type=jnp.float32)
        * attention_score_scale
    )
    positions = lax.broadcasted_iota(jnp.int32, (1, 1, 1, cache_span), 3)
    scores = jnp.where(positions < cache_length[:, None, None, None], scores, -jnp.inf)
    tree_top = jnp.max(tree_score_matrix, axis=-1, keepdims=True)
    largest = jnp.maximum(tree_top, jnp.max(scores, axis=-1, keepdims=True))
    cache_exp = jnp.exp(scores - largest)
    tree_exp = jnp.exp(tree_score_matrix - largest)
    totals = jnp.sum(cache_exp, axis=-1, keepdims=True) + jnp.sum(tree_exp, axis=-1, keepdims=True)
    cache_weights = (cache_exp / totals).astype(jnp.bfloat16)
    tree_weight_matrix = (tree_exp / totals).astype(jnp.bfloat16)
    attention = jnp.einsum(
        "rhnc,rchd->rnhd", cache_weights, values_cache, preferred_element_type=jnp.float32
    )
    attention = attention + jnp.einsum(
        "rhnm,rmhd->rnhd", tree_weight_matrix, tree_value_rows, preferred_element_type=jnp.float32
    )
    head_rows = attention.astype(jnp.bfloat16).reshape(request_count * NODES, device_width)
    node_table = node_rows.reshape(request_count, NODES, 3, device_width)
    chosen = jnp.take_along_axis(node_table, accepted[:, :, None, None], axis=1)
    accepted_kv = jnp.stack([chosen[:, :, 1], chosen[:, :, 2]])
    everything = lax.all_gather(head_rows, "head", axis=0, tiled=True)
    attended = lax.psum_scatter(
        jnp.dot(
            everything[row_tree_nodes], output_weight, preferred_element_type=jnp.float32
        ).astype(jnp.bfloat16),
        "tok",
        scatter_dimension=0,
        tiled=True,
    )
    return (attended, accepted_kv)


def solution(mesh):
    placed = (
        P("tok", None),
        P(),
        P(),
        P("head", None, "tok"),
        P(),
        P("head", None, "tok"),
        P(None, "head", None, "tok"),
        P("head"),
        P("head", None),
        P("head", None),
        P("tok", "head"),
    )
    sized = mesh.shape["head"] == 8 and mesh.shape["tok"] == 4
    return jax.shard_map(
        on_device if sized else plain_on_device,
        mesh=mesh,
        in_specs=placed,
        out_specs=(P("tok", "head"), P(None, "head", None, "tok")),
        check_vma=False,
    )
```
